128 devices in a mesh: dp: 8 (over x, core), label: 16 (over y, z).
Axes of the slice: x: 4, y: 4, z: 4, core: 2. Of those that a mesh axis runs over, the one named last changes fastest.
Arguments:
- queries: bfloat16 [65536, 768], P(('dp', 'label')), may hold values from -6 to 6
- cluster_dest: int32 [65536], P(('dp', 'label')), may hold values from 0 to 4095, as said below
- panels: bfloat16 [2048, 256, 768], P(('dp', 'label')), may hold values from -0.21875 to 0.21875
- scales: bfloat16 [2048, 256], P(('dp', 'label')), may hold values from 0.25 to 4
- shortlist: int32 [128, 24], P(('dp', 'label')), may hold values from 0 to 255, as said below
- positives: int32 [65536, 4], P(('dp', 'label')), may hold values from 0 to 6143
Outputs:
- query_grad: bfloat16 [65536, 768], P(('dp', 'label'))
- panel_grad: bfloat16 [2048, 256, 768], P(('dp', 'label'))
The draws below stay inside these ranges and needn't reach their ends.
Inputs may be any that keep to these rules, and one draw needn't show every extreme that they name: `cluster_dest`: within one label index, the 8 shards' values together take each of 0 to 4095 once; one shard gives one batch a multiple of 32 rows, at most 96, and exactly 96 for some pairs in every draw. `shortlist`: value v of a batch names panel v % 16 of the device with the batch's dp index and label index v // 16; a batch's 24 values are distinct, at most 2 of them share a label index, and exactly 2 do for some label index in every batch.
All inputs are finite; a program needn't handle non-finite values.
Results may differ from the reference program's by a relative error of at most 0.0053.
Values may be sent and summed in bfloat16 or wider, within the bound.
No kernel may reach another device: no remote copies, remote signals or barrier semaphores. Data moves between devices by JAX's collectives and lax.ppermute only.
A program may use at most 192 MiB of HBM per device.

```python
import math
import jax
import jax.numpy as jnp
from jax import lax

D = 768
LANES = 256
Q_DEV = 512
PAN_DEV = 16
CAP = 2
POS = 4
GROUP = 8
OWNERS = 16
SLOTS = 24
QUERIES = 65536
BATCHES = 128
PANELS = 2048


def occurrence(labels, count_total):
    onehot = (labels[:, None] == jnp.arange(count_total, dtype=jnp.int32)[None, :]).astype(jnp.int32)
    return jnp.sum((jnp.cumsum(onehot, axis=0) - 1) * onehot, axis=1)


def shuffled_rows(sub_key):
    return jax.random.permutation(sub_key, Q_DEV).astype(jnp.int32)


def shuffled_panels(sub_key):
    return jax.random.permutation(sub_key, PAN_DEV).astype(jnp.int32)


def group_occurrence(labels):
    return occurrence(labels, GROUP)


def draw_cluster_dest(key, part):
    key = jax.random.fold_in(key, 11)

    def one_column(column_key):
        key_pair, key_rows, key_order = jax.random.split(column_key, 3)
        pairing = jax.random.permutation(key_pair, GROUP).astype(jnp.int32)
        source = jnp.arange(GROUP, dtype=jnp.int32)
        ladder = jnp.arange(GROUP, dtype=jnp.int32)[None, :]
        raised = (pairing[:, None] == ladder).astype(jnp.int32)
        lowered = (pairing[(source + 1) % GROUP][:, None] == ladder).astype(jnp.int32)
        counts = Q_DEV // GROUP + Q_DEV // (2 * GROUP) * (raised - lowered)
        bounds = jnp.cumsum(counts, axis=1)
        row_index = jnp.arange(Q_DEV, dtype=jnp.int32)
        target = jnp.sum((row_index[None, :, None] >= bounds[:, None, :]).astype(jnp.int32), axis=2)
        target = jax.vmap(jax.random.permutation)(jax.random.split(key_rows, GROUP), target).astype(jnp.int32)
        within = jax.vmap(group_occurrence)(target)
        before = jnp.cumsum(counts, axis=0) - counts
        arrival = jnp.take_along_axis(before, target, axis=1) + within
        arrival_order = jax.vmap(shuffled_rows)(jax.random.split(key_order, GROUP))
        position = arrival_order[target, arrival]
        return target * Q_DEV + position
    columns = jax.vmap(one_column)(jax.random.split(key, OWNERS))
    return jnp.transpose(columns, (1, 0, 2)).reshape(-1).astype(jnp.int32)


def draw_shortlist(key, part):
    key = jax.random.fold_in(key, 23)

    def one_batch(batch_key):
        key_lead, key_spare, key_mix, key_local = jax.random.split(batch_key, 4)
        leader = jax.random.randint(key_lead, (), 0, OWNERS).astype(jnp.int32)
        spares = (leader + 1 + jnp.arange((OWNERS - 1) * CAP, dtype=jnp.int32) // CAP) % OWNERS
        spares = jax.random.permutation(key_spare, spares)
        owners = jnp.concatenate([jnp.full((CAP,), 0, jnp.int32) + leader, spares[:SLOTS - CAP].astype(jnp.int32)])
        owners = jax.random.permutation(key_mix, owners)
        within = occurrence(owners, OWNERS)
        table_local = jax.vmap(shuffled_panels)(jax.random.split(key_local, OWNERS))
        return owners * PAN_DEV + table_local[owners, within]
    return jax.vmap(one_batch)(jax.random.split(key, BATCHES)).astype(jnp.int32)


def touch_ends(entries, key, low, largest):
    spot = [jax.random.randint(jax.random.fold_in(key, axis), (), 0, length) for axis, length in enumerate(entries.shape)]
    longest = entries.shape.index(max(entries.shape))
    neighbour = spot[:longest] + [(spot[longest] + 1) % entries.shape[longest]] + spot[longest + 1:]
    return entries.at[tuple(spot)].set(low).at[tuple(neighbour)].set(largest)


def block_levels(rng, extent, pieces, least, top_value):
    def one(axis_at, shards_of):
        draws = jax.random.uniform(jax.random.fold_in(jax.random.fold_in(rng, 6), axis_at), (shards_of,), jnp.float32, least / len(pieces), top_value / len(pieces))
        return jnp.repeat(jnp.exp(draws), extent[axis_at] // shards_of).reshape((-1,) + (1,) * (len(extent) - axis_at - 1))

    level = one(*pieces[0])
    for cut in pieces[1:]:
        level = level * one(*cut)
    return level


def scatter_about(key, dims, scale, most, pieces=(), kind=jnp.bfloat16):
    array = jax.random.normal(key, dims, jnp.float32) * scale
    if len(pieces) > 0:
        array = block_levels(key, dims, pieces, -0.22, 0.18) * array
    return jnp.clip(array, min=-most, max=most).astype(kind)


def setup_inputs(seed: int = 0) -> dict:
    key_list = jax.random.split(jax.random.key(seed), 7)
    queries = scatter_about(key_list[0], (QUERIES, D), 1.0, 6.0, ((0, 128),))
    cluster_dest = draw_cluster_dest(jax.random.fold_in(key_list[6], 71), 0)
    panels = scatter_about(key_list[2], (PANELS, LANES, D), D ** -0.5, 0.21875, ((0, 128),))
    scales = jnp.clip(jnp.exp(math.log(4.0) - 2.7725887 * jax.random.uniform(key_list[3], (PANELS, LANES), jnp.float32) ** block_levels(key_list[3], (PANELS, LANES), ((0, 128),), -0.2, 0.2)), 0.25, 4.0).astype(jnp.bfloat16)
    shortlist = draw_shortlist(jax.random.fold_in(key_list[6], 71), 0)
    positives = touch_ends(jax.random.randint(key_list[5], (QUERIES, POS), 0, SLOTS * LANES), jax.random.fold_in(key_list[5], 1), 0, (SLOTS * LANES) - 1).astype(jnp.int32)
    return {"queries": queries, "cluster_dest": cluster_dest, "panels": panels, "scales": scales, "shortlist": shortlist, "positives": positives}


def label_hits(batch_pos, label_ids):
    return jnp.any(batch_pos[:, :, None, None] == label_ids[None, None, :, :], axis=1).astype(jnp.float32)


def place_rows(column_rows, where_to):
    return jnp.zeros_like(column_rows).at[where_to].set(column_rows)


def take_rows(column_rows, where_to):
    return column_rows[where_to]


def reference(queries, cluster_dest, panels, scales, shortlist, positives):
    blocks = queries.reshape(GROUP, OWNERS, Q_DEV, D)
    dest_blocks = cluster_dest.reshape(GROUP, OWNERS, Q_DEV)
    column_rows = jnp.transpose(blocks, (1, 0, 2, 3)).reshape(OWNERS, GROUP * Q_DEV, D)
    column_dest = jnp.transpose(dest_blocks, (1, 0, 2)).reshape(OWNERS, GROUP * Q_DEV).astype(jnp.int32)
    clustered = jax.vmap(place_rows)(column_rows, column_dest)
    batches = jnp.transpose(clustered.reshape(OWNERS, GROUP, Q_DEV, D), (1, 0, 2, 3))
    row_panels = panels.reshape(GROUP, OWNERS * PAN_DEV, LANES, D)
    row_scales = scales.reshape(GROUP, OWNERS * PAN_DEV, LANES)
    list_rows = shortlist.reshape(GROUP, OWNERS, SLOTS).astype(jnp.int32)
    pos_rows = positives.reshape(GROUP, OWNERS, Q_DEV, POS)
    label_ids = jnp.arange(SLOTS, dtype=jnp.int32)[:, None] * LANES + jnp.arange(LANES, dtype=jnp.int32)[None, :]

    def one_row(row_items):
        row_batches, row_lists, row_pos, panel_here, scale_here = row_items

        def one_batch(grad_total, batch_items):
            batch_input_rows, wanted, batch_pos = batch_items
            selected_panel = panel_here[wanted].astype(jnp.float32)
            selected_scale = scale_here[wanted].astype(jnp.float32)
            label_scores = jnp.einsum("rp,wjp->rwj", batch_input_rows.astype(jnp.float32), selected_panel) * selected_scale[None]
            error_signal = ((jax.nn.sigmoid(label_scores) - label_hits(batch_pos, label_ids)) * selected_scale[None]).astype(jnp.bfloat16)
            error_signal = lax.optimization_barrier(error_signal).astype(jnp.float32)
            batch_gradient_total = jnp.einsum("rzp,zpc->rc", error_signal, selected_panel).astype(jnp.bfloat16)
            gradient_share = jnp.einsum("zbt,zp->btp", error_signal, batch_input_rows.astype(jnp.float32)).astype(jnp.bfloat16)
            gradient_share = lax.optimization_barrier(gradient_share)
            return grad_total.at[wanted].add(gradient_share.astype(jnp.float32)), batch_gradient_total

        start_total = jnp.zeros((OWNERS * PAN_DEV, LANES, D), jnp.float32)
        grad_total, batch_grads = lax.scan(one_batch, start_total, (row_batches, row_lists, row_pos))
        return grad_total.astype(jnp.bfloat16), batch_grads

    panel_grad, batch_grads = lax.map(one_row, (batches, list_rows, pos_rows, row_panels, row_scales))
    clustered_grads = jnp.transpose(batch_grads, (1, 0, 2, 3)).reshape(OWNERS, GROUP * Q_DEV, D)
    home_rows = jax.vmap(take_rows)(clustered_grads, column_dest)
    query_grad = jnp.transpose(home_rows.reshape(OWNERS, GROUP, Q_DEV, D), (1, 0, 2, 3)).reshape(GROUP * OWNERS * Q_DEV, D)
    return query_grad, panel_grad.reshape(GROUP * OWNERS * PAN_DEV, LANES, D)
```

```python
import functools
import jax
import jax.numpy as jnp
from jax import lax
from jax.experimental import pallas as pl
from jax.experimental.pallas import tpu as pltpu
from jax.sharding import PartitionSpec as P

CAP = 2
CODE = 16
BF = jnp.bfloat16
F32 = jnp.float32


def iota(shape, axis):
    return lax.broadcasted_iota(jnp.int32, shape, axis)


def dot(a, b, dims):
    return lax.dot_general(a, b, (dims, ((), ())), preferred_element_type=F32)


NN = ((1,), (0,))
NT = ((1,), (1,))
TN = ((0,), (0,))


def params(limit):
    return pltpu.CompilerParams(vmem_limit_bytes=limit)


def pack_body(groups, slots, x_ref, dest_ref, out_ref, rank_ref):
    rows = x_ref.shape[0]
    dest = dest_ref[...]
    target = dest // rows
    place = dest % rows
    member = jnp.where(iota((16, rows), 0) == target, 1.0, 0.0)
    earlier = jnp.where(iota((rows, rows), 0) < iota((rows, rows), 1), 1.0, 0.0).astype(BF)
    rank = jnp.sum(dot(member.astype(BF), earlier, NN) * member, axis=0, keepdims=True)
    rank = rank.astype(jnp.int32)
    rank_ref[...] = rank + target * slots
    kind = iota((CODE, rows), 0)
    code = jnp.where(kind == 0, place // 16, jnp.where(kind == 1, place % 16, 1))
    code = code.astype(F32).astype(BF)
    out_ref[:, slots:, :] = jnp.zeros((groups, CODE, x_ref.shape[1]), BF)
    for t in range(groups):
        pick = jnp.where(iota((slots, rows), 0) == jnp.where(target == t, rank, -1), 1.0, 0.0).astype(BF)
        out_ref[t, :slots, :] = dot(pick, x_ref[...], NN).astype(BF)
        out_ref[t, slots:, :slots] = dot(code, pick, NT).astype(BF)


def pack(x, dest, groups, slots):
    rows, width = x.shape
    return pl.pallas_call(
        functools.partial(pack_body, groups, slots),
        out_shape=(
            jax.ShapeDtypeStruct((groups, slots + CODE, width), BF),
            jax.ShapeDtypeStruct((1, rows), jnp.int32),
        ),
        compiler_params=params(32 << 20),
        name="pack_rows",
    )(x, dest)


def places(coded, slots):
    code = coded[:, :slots].astype(F32)
    place = (code[0:1] * 16.0 + code[1:2]).astype(jnp.int32)
    return jnp.where(code[2:3] > 0.5, place, -1)


def land_body(groups, slots, arrived_ref, code_ref, out_ref, place_ref):
    rows = out_ref.shape[0] - CODE
    total = jnp.zeros((rows, out_ref.shape[1]), F32)
    for s in range(groups):
        place = places(arrived_ref[s, slots:, :], slots)
        place_ref[s : s + 1, :] = place
        put = jnp.where(iota((rows, slots), 0) == place, 1.0, 0.0).astype(BF)
        total += dot(put, arrived_ref[s, :slots, :], NN)
    out_ref[:rows, :] = total.astype(BF)
    out_ref[rows:, :] = code_ref[...]


def land(arrived, code, rows, slots):
    groups, _, width = arrived.shape
    return pl.pallas_call(
        functools.partial(land_body, groups, slots),
        out_shape=(
            jax.ShapeDtypeStruct((rows + CODE, width), BF),
            jax.ShapeDtypeStruct((groups, slots), jnp.int32),
        ),
        compiler_params=params(32 << 20),
        name="land_rows",
    )(arrived, code)


def leave_body(groups, slots, grad_ref, place_ref, out_ref):
    rows = grad_ref.shape[0]
    for s in range(groups):
        put = jnp.where(iota((rows, slots), 0) == place_ref[s : s + 1, :], 1.0, 0.0).astype(BF)
        out_ref[s] = dot(put, grad_ref[...], TN).astype(BF)


def leave(grad, place):
    groups, slots = place.shape
    return pl.pallas_call(
        functools.partial(leave_body, groups, slots),
        out_shape=jax.ShapeDtypeStruct((groups, slots, grad.shape[1]), BF),
        compiler_params=params(32 << 20),
        name="leave_rows",
    )(grad, place)


def home_body(groups, slots, back_ref, rank_ref, out_ref):
    rows = out_ref.shape[0]
    total = jnp.zeros(out_ref.shape, F32)
    for t in range(groups):
        pick = jnp.where(iota((slots, rows), 0) + t * slots == rank_ref[...], 1.0, 0.0).astype(BF)
        total += dot(pick, back_ref[t], TN)
    out_ref[...] = total.astype(BF)


def home(back, rank):
    groups, slots, width = back.shape
    return pl.pallas_call(
        functools.partial(home_body, groups, slots),
        out_shape=jax.ShapeDtypeStruct((rank.shape[1], width), BF),
        compiler_params=params(32 << 20),
        name="home_rows",
    )(back, rank)


def work_body(table_ref, x_ref, w_ref, scale_ref, part_ref, grad_ref, total_ref, lane_scale_ref):
    b = pl.program_id(0)
    count, lanes, width = w_ref.shape
    rows = part_ref.shape[1]

    @pl.when(b == 0)
    def _():
        total_ref[...] = jnp.zeros(total_ref.shape, F32)
        columns = jnp.transpose(scale_ref[...].astype(F32))
        for p in range(count):
            lane_scale_ref[p] = jnp.broadcast_to(columns[:, p : p + 1], (lanes, 128))

    x = x_ref[0, :rows, :]
    code = x_ref[0, rows:, :rows].astype(F32).astype(jnp.int32)

    def one(c):
        slot = table_ref[b, 2 * c]
        panel = table_ref[b, 2 * c + 1]
        w = w_ref[panel]
        scale = jnp.concatenate([lane_scale_ref[panel]] * (rows // 128), axis=1)
        score = dot(w, x, NT) * scale
        lane = iota((lanes, rows), 0)
        hit = lane == jnp.where(code[0:1] == slot, code[4:5], -1)
        for k in range(1, 4):
            hit |= lane == jnp.where(code[k : k + 1] == slot, code[4 + k : 5 + k], -1)
        signal = ((jax.nn.sigmoid(score) - jnp.where(hit, 1.0, 0.0)) * scale).astype(BF)
        total_ref[panel] += dot(signal, x, NN)
        return dot(signal, w, TN)

    first = table_ref[b, 0] >= 0
    second = table_ref[b, 2] >= 0

    @pl.when(jnp.logical_not(first))
    def _():
        part_ref[...] = jnp.zeros(part_ref.shape, BF)

    @pl.when(first & jnp.logical_not(second))
    def _():
        part_ref[0] = one(0).astype(BF)

    @pl.when(second)
    def _():
        part_ref[0] = (one(0) + one(1)).astype(BF)

    @pl.when(b == pl.num_programs(0) - 1)
    def _():
        grad_ref[...] = total_ref[...].astype(BF)


def work(table, x, panels, scales):
    batches, long_rows, width = x.shape
    rows = long_rows - CODE
    count, lanes, _ = panels.shape
    once = pl.Buffered(1)
    return pl.pallas_call(
        work_body,
        grid_spec=pltpu.PrefetchScalarGridSpec(
            num_scalar_prefetch=1,
            grid=(batches,),
            in_specs=[
                pl.BlockSpec((1, long_rows, width), lambda b, t: (b, 0, 0)),
                pl.BlockSpec((count, lanes, width), lambda b, t: (0, 0, 0), pipeline_mode=once),
                pl.BlockSpec((count, lanes), lambda b, t: (0, 0)),
            ],
            out_specs=[
                pl.BlockSpec((1, rows, width), lambda b, t: (b, 0, 0)),
                pl.BlockSpec((count, lanes, width), lambda b, t: (0, 0, 0)),
            ],
            scratch_shapes=[
                pltpu.VMEM((count, lanes, width), F32),
                pltpu.VMEM((count, lanes, 128), F32),
            ],
        ),
        out_shape=(
            jax.ShapeDtypeStruct((batches, rows, width), BF),
            jax.ShapeDtypeStruct(panels.shape, BF),
        ),
        compiler_params=params(58 << 20),
        name="owner_work",
    )(table, x, panels, scales)


def shards(queries, cluster_dest, panels, scales, shortlist, positives):
    rows, width = queries.shape
    count, lanes = scales.shape
    groups = lax.axis_size("dp")
    owners = lax.axis_size("label")
    slots = 3 * rows // (2 * groups)

    wanted = shortlist[0]
    slot_total = wanted.shape[0]
    slot_ids = jnp.arange(slot_total, dtype=jnp.int32)[None, :]
    mine = (wanted // count)[None, :] == jnp.arange(owners, dtype=jnp.int32)[:, None]
    first = jnp.min(jnp.where(mine, slot_ids, slot_total), axis=1, keepdims=True)
    last = jnp.max(jnp.where(mine, slot_ids, -1), axis=1, keepdims=True)
    local = (wanted % count)[None, :]
    first_panel = jnp.max(jnp.where(slot_ids == first, local, -1), axis=1, keepdims=True)
    last_panel = jnp.max(jnp.where(slot_ids == last, local, -1), axis=1, keepdims=True)
    none = first_panel < 0
    single = last == first
    request = jnp.concatenate(
        [
            jnp.where(none, -1, first),
            first_panel,
            jnp.where(none | single, -1, last),
            jnp.where(none | single, -1, last_panel),
        ],
        axis=1,
    )
    table = lax.all_to_all(request, "label", split_axis=0, concat_axis=0, tiled=True)

    marks = positives.T
    code = jnp.concatenate([marks // lanes, marks % lanes], axis=0).astype(F32).astype(BF)
    code = jnp.pad(code, ((0, CODE - code.shape[0]), (0, width - rows)))

    outgoing, rank = pack(queries, cluster_dest.reshape(1, rows), groups, slots)
    arrived = lax.all_to_all(outgoing, "dp", split_axis=0, concat_axis=0, tiled=True)
    batch, place = land(arrived, code, rows, slots)
    gathered = lax.all_gather(batch, "label")
    part, panel_grad = work(table, gathered, panels, scales)
    grad = lax.psum_scatter(part, "label", scatter_dimension=0, tiled=False)
    back = lax.all_to_all(leave(grad, place), "dp", split_axis=0, concat_axis=0, tiled=True)
    return home(back, rank), panel_grad


def solution(mesh):
    placed = (
        P(("dp", "label"), None),
        P(("dp", "label")),
        P(("dp", "label"), None, None),
        P(("dp", "label"), None),
        P(("dp", "label"), None),
        P(("dp", "label"), None),
    )
    return jax.shard_map(
        shards,
        mesh=mesh,
        in_specs=placed,
        out_specs=(P(("dp", "label"), None), P(("dp", "label"), None, None)),
        check_vma=False,
    )
```

```python
import functools
import jax
import jax.numpy as jnp
from jax import lax
from jax.experimental import pallas as pl
from jax.experimental.pallas import tpu as pltpu
from jax.sharding import PartitionSpec as P

CAP = 2
CODE = 16
LIMIT = 60 << 20
BF = jnp.bfloat16
F32 = jnp.float32


def iota(shape, axis):
    return lax.broadcasted_iota(jnp.int32, shape, axis)


def dot(a, b, dims):
    return lax.dot_general(a, b, (dims, ((), ())), preferred_element_type=F32)


NN = ((1,), (0,))
NT = ((1,), (1,))
TN = ((0,), (0,))


def params(limit):
    return pltpu.CompilerParams(vmem_limit_bytes=limit)


def pack_body(groups, slots, x_ref, dest_ref, out_ref, rank_ref):
    rows = x_ref.shape[0]
    dest = dest_ref[...]
    target = dest // rows
    place = dest % rows
    member = jnp.where(iota((16, rows), 0) == target, 1.0, 0.0)
    earlier = jnp.where(iota((rows, rows), 0) < iota((rows, rows), 1), 1.0, 0.0).astype(BF)
    rank = jnp.sum(dot(member.astype(BF), earlier, NN) * member, axis=0, keepdims=True)
    rank = rank.astype(jnp.int32)
    rank_ref[...] = rank + target * slots
    kind = iota((CODE, rows), 0)
    code = jnp.where(kind == 0, place // 16, jnp.where(kind == 1, place % 16, 1))
    code = code.astype(F32).astype(BF)
    out_ref[:, slots:, :] = jnp.zeros((groups, CODE, x_ref.shape[1]), BF)
    for t in range(groups):
        pick = jnp.where(iota((slots, rows), 0) == jnp.where(target == t, rank, -1), 1.0, 0.0).astype(BF)
        out_ref[t, :slots, :] = dot(pick, x_ref[...], NN).astype(BF)
        out_ref[t, slots:, :slots] = dot(code, pick, NT).astype(BF)


def pack(x, dest, groups, slots):
    rows, width = x.shape
    return pl.pallas_call(
        functools.partial(pack_body, groups, slots),
        out_shape=(
            jax.ShapeDtypeStruct((groups, slots + CODE, width), BF),
            jax.ShapeDtypeStruct((1, rows), jnp.int32),
        ),
        compiler_params=params(LIMIT),
        name="pack_rows",
    )(x, dest)


def places(coded, slots):
    code = coded[:, :slots].astype(F32)
    place = (code[0:1] * 16.0 + code[1:2]).astype(jnp.int32)
    return jnp.where(code[2:3] > 0.5, place, -1)


def land_body(groups, slots, arrived_ref, place_ref, *pair_refs):
    part = pair_refs[0].shape[1]
    rows = 2 * part * len(pair_refs)
    total = jnp.zeros((rows, arrived_ref.shape[2]), F32)
    for s in range(groups):
        place = places(arrived_ref[s, slots:, :], slots)
        place_ref[s : s + 1, :] = place
        put = jnp.where(iota((rows, slots), 0) == place, 1.0, 0.0).astype(BF)
        total += dot(put, arrived_ref[s, :slots, :], NN)
    for k in range(2 * len(pair_refs)):
        pair_refs[k // 2][k % 2] = total[k * part : (k + 1) * part].astype(BF)


def land(arrived, rows, slots):
    groups, _, width = arrived.shape
    pair = jax.ShapeDtypeStruct((2, rows // STREAMS, width), BF)
    return pl.pallas_call(
        functools.partial(land_body, groups, slots),
        out_shape=(jax.ShapeDtypeStruct((groups, slots), jnp.int32), pair, pair),
        compiler_params=params(LIMIT),
        name="land_rows",
    )(arrived)


def leave_body(groups, slots, terms, *refs):
    place_ref, out_ref = refs[0], refs[-1]
    streams = []
    for k in range(STREAMS):
        total = refs[1 + k * terms][0].astype(F32)
        for ref in refs[2 + k * terms : 1 + (k + 1) * terms]:
            total += ref[0].astype(F32)
        streams.append(total.astype(BF))
    grad = jnp.concatenate(streams, axis=0)
    rows = grad.shape[0]
    for s in range(groups):
        put = jnp.where(iota((rows, slots), 0) == place_ref[s : s + 1, :], 1.0, 0.0).astype(BF)
        out_ref[s] = dot(put, grad, TN).astype(BF)


def one_block(array, index, part):
    _, rows, width = array.shape
    return pl.BlockSpec((1, part, width), lambda i: (index, i, 0))


def leave(place, terms):
    groups, slots = place.shape
    flat = [term for stream in terms for term in stream]
    width = flat[0][0].shape[2]
    return pl.pallas_call(
        functools.partial(leave_body, groups, slots, len(terms[0])),
        grid=(1,),
        in_specs=[pl.BlockSpec((groups, slots), lambda i: (0, 0))]
        + [one_block(a, index, a.shape[1]) for a, index in flat],
        out_specs=pl.BlockSpec((groups, slots, width), lambda i: (0, 0, 0)),
        out_shape=jax.ShapeDtypeStruct((groups, slots, width), BF),
        compiler_params=params(LIMIT),
        name="leave_rows",
    )(place, *[a for a, _ in flat])


def merge_body(sums, *refs):
    outs = refs[-STREAMS:]
    at = 0
    for k, blocks in enumerate(sums):
        for j, terms in enumerate(blocks):
            total = refs[at][0].astype(F32)
            for ref in refs[at + 1 : at + len(terms)]:
                total += ref[0].astype(F32)
            outs[k][j] = total.astype(BF)
            at += len(terms)


def merge(sums, name):
    flat = [term for blocks in sums for terms in blocks for term in terms]
    _, rows, width = flat[0][0].shape
    count = len(sums[0])
    steps = 2
    part = rows // steps
    return pl.pallas_call(
        functools.partial(merge_body, [[[0] * len(t) for t in b] for b in sums]),
        grid=(steps,),
        in_specs=[one_block(a, index, part) for a, index in flat],
        out_specs=[pl.BlockSpec((count, part, width), lambda i: (0, i, 0))] * STREAMS,
        out_shape=[jax.ShapeDtypeStruct((count, rows, width), BF)] * STREAMS,
        compiler_params=params(LIMIT),
        cost_estimate=pl.CostEstimate(
            flops=0, transcendentals=0, bytes_accessed=2 * rows * width * (len(flat) + count * STREAMS)
        ),
        name=name,
    )(*[a for a, _ in flat])


def home_body(groups, slots, back_ref, rank_ref, out_ref):
    rows = out_ref.shape[0]
    total = jnp.zeros(out_ref.shape, F32)
    for t in range(groups):
        pick = jnp.where(iota((slots, rows), 0) + t * slots == rank_ref[...], 1.0, 0.0).astype(BF)
        total += dot(pick, back_ref[t], TN)
    out_ref[...] = total.astype(BF)


def home(back, rank):
    groups, slots, width = back.shape
    return pl.pallas_call(
        functools.partial(home_body, groups, slots),
        out_shape=jax.ShapeDtypeStruct((rank.shape[1], width), BF),
        compiler_params=params(LIMIT),
        name="home_rows",
    )(back, rank)


def work_body(units, n_in, n_out, *refs):
    table_ref, meta_ref, code_ref, w_hbm, scale_ref = refs[:5]
    x_refs = refs[5 : 5 + n_in]
    out_refs = refs[5 + n_in : 5 + n_in + n_out]
    signal_ref = refs[5 + n_in + n_out]
    scratch = refs[6 + n_in + n_out :]
    x_buf, out_buf, signal_buf, w_ref, lane_scale_ref, ready_ref, in_sem, out_sem, signal_sem, w_sem = scratch
    total = len(units)
    count, lanes, width = w_ref.shape
    rows = x_buf.shape[1]
    part = rows // 2

    def store(u):
        copies = [pltpu.make_async_copy(signal_buf.at[u], signal_ref.at[u], signal_sem.at[u])]
        for h, (array, block) in enumerate(units[u][1]):
            cut = out_buf.at[u, pl.ds(h * part, part)]
            copies.append(pltpu.make_async_copy(cut, out_refs[array].at[block], out_sem.at[2 * u + h]))
        return copies

    def fetch(u):
        for h, (array, index) in enumerate(units[u][0]):
            cut = x_buf.at[u, pl.ds(h * part, part)]
            pltpu.make_async_copy(x_refs[array].at[index], cut, in_sem.at[u]).start()

    def panel_copy(p):
        return pltpu.make_async_copy(w_hbm.at[p], w_ref.at[p], w_sem.at[p])

    fetch(0)
    for p in range(count):
        panel_copy(p).start()
        ready_ref[p] = 0
    for u in range(1, total):
        fetch(u)
    columns = jnp.transpose(scale_ref[...].astype(F32))
    for p in range(count):
        lane_scale_ref[p] = jnp.broadcast_to(columns[:, p : p + 1], (lanes, 128))

    def need(panel):
        @pl.when(ready_ref[panel] == 0)
        def _():
            panel_copy(panel).wait()
            ready_ref[panel] = 1

    def unit(u, carry):
        pltpu.make_async_copy(x_buf.at[u], x_buf.at[u], in_sem.at[u]).wait()
        batch = meta_ref[0, u]
        x = x_buf[u]
        code = code_ref[batch, meta_ref[1, u]].astype(F32).astype(jnp.int32)

        def one(c):
            slot = table_ref[batch, 2 * c]
            panel = table_ref[batch, 2 * c + 1]
            w = w_ref[panel]
            scale = jnp.concatenate([lane_scale_ref[panel]] * (rows // 128), axis=1)
            score = dot(w, x, NT) * scale
            lane = iota((lanes, rows), 0)
            hit = lane == jnp.where(code[0:1] == slot, code[4:5], -1)
            for k in range(1, 4):
                hit |= lane == jnp.where(code[k : k + 1] == slot, code[4 + k : 5 + k], -1)
            signal = ((jax.nn.sigmoid(score) - jnp.where(hit, 1.0, 0.0)) * scale).astype(BF)
            signal_buf[u, c] = signal
            return dot(signal, w, TN)

        first = table_ref[batch, 0] >= 0
        second = table_ref[batch, 2] >= 0

        @pl.when(jnp.logical_not(first))
        def _():
            out_buf[u] = jnp.zeros((rows, width), BF)

        @pl.when(first & jnp.logical_not(second))
        def _():
            need(table_ref[batch, 1])
            out_buf[u] = one(0).astype(BF)

        @pl.when(second)
        def _():
            need(table_ref[batch, 1])
            need(table_ref[batch, 3])
            out_buf[u] = (one(0) + one(1)).astype(BF)

        for v in range(total):

            @pl.when(u == v)
            def _():
                for copy in store(v):
                    copy.start()

        return carry

    lax.fori_loop(0, total, unit, 0)
    for p in range(count):
        need(p)
    for u in range(total):
        for copy in store(u):
            copy.wait()


def work(table, batches, codes, panels, scales, arrays, units, out_blocks, name):
    count, lanes, width = panels.shape
    part = codes.shape[3] // 2
    rows = 2 * part
    meta = jnp.stack([batches, jnp.array([u[2] for u in units], jnp.int32)])
    total = len(units)
    whole = pl.BlockSpec(memory_space=pltpu.VMEM)
    scalar = pl.BlockSpec(memory_space=pltpu.SMEM)
    loose = pl.BlockSpec(memory_space=pltpu.HBM)
    outs = pl.pallas_call(
        functools.partial(work_body, units, len(arrays), len(out_blocks)),
        in_specs=[scalar, scalar, whole, loose, whole] + [loose] * len(arrays),
        out_specs=[loose] * len(out_blocks) + [loose],
        out_shape=[jax.ShapeDtypeStruct((n, part, width), BF) for n in out_blocks]
        + [jax.ShapeDtypeStruct((total, CAP, lanes, rows), BF)],
        scratch_shapes=[
            pltpu.VMEM((total, rows, width), BF),
            pltpu.VMEM((total, rows, width), BF),
            pltpu.VMEM((total, CAP, lanes, rows), BF),
            pltpu.VMEM(panels.shape, BF),
            pltpu.VMEM((count, lanes, 128), F32),
            pltpu.SMEM((count,), jnp.int32),
            pltpu.SemaphoreType.DMA((total,)),
            pltpu.SemaphoreType.DMA((2 * total,)),
            pltpu.SemaphoreType.DMA((total,)),
            pltpu.SemaphoreType.DMA((count,)),
        ],
        compiler_params=params(LIMIT),
        cost_estimate=pl.CostEstimate(
            flops=total * 3 * lanes * rows * width * 4,
            transcendentals=0,
            bytes_accessed=panels.size * 2 + total * rows * (width * 4 + lanes * 2),
        ),
        name=name,
    )(table, meta, codes, panels, scales, *arrays)
    return outs[:-1], outs[-1]


def panel_body(parts, n_arrays, n_signals, *refs):
    table_ref, batch_ref = refs[:2]
    x_refs = refs[2 : 2 + n_arrays]
    s_refs = refs[2 + n_arrays : 2 + n_arrays + n_signals]
    grad_ref, x_all, s_all, total_ref, x_sem, s_sem = refs[2 + n_arrays + n_signals :]
    rows = x_all.shape[1] // STREAMS
    for rel, pieces in enumerate(parts):
        for pair, (sources, signal, unit) in enumerate(pieces):
            wide = pl.ds(2 * pair * rows, 2 * rows)
            for h, (array, index) in enumerate(sources):
                cut = pl.ds((2 * pair + h) * rows, rows)
                pltpu.make_async_copy(x_refs[array].at[index], x_all.at[rel, cut], x_sem.at[rel]).start()
            pltpu.make_async_copy(s_refs[signal].at[unit], s_all.at[rel, :, :, wide], s_sem.at[rel]).start()
    total_ref[...] = jnp.zeros(total_ref.shape, F32)

    def batch(rel, carry):
        pltpu.make_async_copy(x_all.at[rel], x_all.at[rel], x_sem.at[rel]).wait()
        pltpu.make_async_copy(s_all.at[rel], s_all.at[rel], s_sem.at[rel]).wait()
        for c in range(CAP):
            panel = table_ref[batch_ref[rel], 2 * c + 1]

            @pl.when(panel >= 0)
            def _():
                total_ref[panel] += dot(s_all[rel, c], x_all[rel], NN)

        return carry

    lax.fori_loop(0, len(parts), batch, 0)
    grad_ref[...] = total_ref[...].astype(BF)


def panel_sum(table, batches, arrays, signals, parts, shape):
    count, lanes, width = shape
    rows = arrays[0].shape[2] * STREAMS
    scalar = pl.BlockSpec(memory_space=pltpu.SMEM)
    loose = pl.BlockSpec(memory_space=pltpu.HBM)
    return pl.pallas_call(
        functools.partial(panel_body, parts, len(arrays), len(signals)),
        in_specs=[scalar, scalar] + [loose] * (len(arrays) + len(signals)),
        out_specs=pl.BlockSpec(memory_space=pltpu.VMEM),
        out_shape=jax.ShapeDtypeStruct(shape, BF),
        scratch_shapes=[
            pltpu.VMEM((len(parts), rows, width), BF),
            pltpu.VMEM((len(parts), CAP, lanes, rows), BF),
            pltpu.VMEM(shape, F32),
            pltpu.SemaphoreType.DMA((len(parts),)),
            pltpu.SemaphoreType.DMA((len(parts),)),
        ],
        compiler_params=params(LIMIT),
        cost_estimate=pl.CostEstimate(
            flops=len(parts) * CAP * lanes * rows * width * 2,
            transcendentals=0,
            bytes_accessed=len(parts) * rows * (width + CAP * lanes) * 2 + count * lanes * width * 2,
        ),
        name="panel_grad",
    )(table, batches, *arrays, *signals)


ORDERS = ((1, 3, 4, 12), (3, 1, 12, 4), (4, 12, 1, 3), (12, 4, 3, 1))
STREAMS = len(ORDERS)
RINGS = ((1, 3), (4, 12))


def swap(array, mask, owners):
    return lax.ppermute(array, "label", [(i, i ^ mask) for i in range(owners)])


def shards(queries, cluster_dest, panels, scales, shortlist, positives):
    rows, width = queries.shape
    count, lanes = scales.shape
    groups = lax.axis_size("dp")
    owners = lax.axis_size("label")
    slots = 3 * rows // (2 * groups)
    part = rows // STREAMS
    me = lax.axis_index("label").astype(jnp.int32)

    marks = positives.T
    code = jnp.concatenate([marks // lanes, marks % lanes], axis=0).astype(F32).astype(BF)
    wanted_row = jnp.pad(shortlist.astype(F32).astype(BF), ((0, 0), (0, rows - shortlist.shape[1])))
    code = jnp.concatenate([code, wanted_row, jnp.zeros((CODE - code.shape[0] - 1, rows), BF)], axis=0)
    codes = lax.all_to_all(
        jnp.broadcast_to(code, (owners, *code.shape)), "label", split_axis=0, concat_axis=0, tiled=True
    )
    wanted = codes[:, 8, : shortlist.shape[1]].astype(F32).astype(jnp.int32)
    codes = jnp.transpose(codes.reshape(owners, CODE, STREAMS // 2, 2 * part), (0, 2, 1, 3))
    slot_ids = jnp.arange(wanted.shape[1], dtype=jnp.int32)[None, :]
    mine = wanted // count == me
    local = wanted % count
    first = jnp.min(jnp.where(mine, slot_ids, wanted.shape[1]), axis=1, keepdims=True)
    last = jnp.max(jnp.where(mine, slot_ids, -1), axis=1, keepdims=True)
    first_panel = jnp.max(jnp.where(slot_ids == first, local, -1), axis=1, keepdims=True)
    last_panel = jnp.max(jnp.where(slot_ids == last, local, -1), axis=1, keepdims=True)
    none = first_panel < 0
    single = none | (last == first)
    table = jnp.concatenate(
        [
            jnp.where(none, -1, first),
            first_panel,
            jnp.where(single, -1, last),
            jnp.where(single, -1, last_panel),
        ],
        axis=1,
    )

    outgoing, rank = pack(queries, cluster_dest.reshape(1, rows), groups, slots)
    arrived = lax.all_to_all(outgoing, "dp", split_axis=0, concat_axis=0, tiled=True)
    place, *own = land(arrived, rows, slots)

    every = range(STREAMS)
    order = ORDERS
    arrays = []
    for pair, (one, three) in zip(own, RINGS):
        by1, by3 = swap(pair, one, owners), swap(pair, three, owners)
        low, high = swap(by1[0], three, owners), swap(by3[1], one, owners)
        near = jnp.stack([pair, by1, jnp.stack([low, high]), by3], axis=1)
        arrays.append([near])
    for group, (one, three) in zip(arrays, RINGS[::-1]):
        by1, by3 = swap(group[0], one, owners), swap(group[0], three, owners)
        group += [by1, by3, swap(by1[0], three, owners), swap(by3[1], one, owners)]

    def rel(k, bits):
        out = 0
        for s in range(4):
            if bits >> s & 1:
                out ^= order[k][s]
        return out

    where = {}

    def bits_of(k, r):
        return next(b for b in range(owners) if rel(k, b) == r)

    def stage(name, index, members):
        outs_of, units, ids, used = {}, [], [], []

        def source(array):
            if array not in used:
                used.append(array)
            return used.index(array)

        for pair, far, spot in members:
            r = 4 * far + spot if pair == 0 else 4 * spot + far
            legs = [(k, bits_of(k, r)) for k in (2 * pair, 2 * pair + 1)]
            if far == 2:
                origin = (((pair, 3), spot), ((pair, 4), spot))
            else:
                array = (pair, (0, 1, None, 2)[far])
                origin = ((array, (0, spot)), (array, (1, spot)))
            for k, b in legs:
                outs_of.setdefault((k, b & 1), []).append(b)
            where[pair, r] = (origin, index, len(units))
            units.append((tuple((source(a), i) for a, i in origin), legs, pair))
            ids.append(r)
        keys = sorted(outs_of)
        for key in keys:
            outs_of[key].sort(key=lambda b: (b >> 1 & 1, b))
        units = [
            (origin, tuple((keys.index((k, b & 1)), outs_of[k, b & 1].index(b)) for k, b in legs), pair)
            for origin, legs, pair in units
        ]
        batches = jnp.array(ids, jnp.int32) ^ me
        blocks = [len(outs_of[key]) for key in keys]
        ins = [arrays[pair][a] for pair, a in used]
        outs, signals = work(table, batches, codes, panels, scales, ins, units, blocks, name)
        outs = dict(zip(keys, outs))
        for key in keys:
            for n, b in enumerate(outs_of[key]):
                made[key[0], b] = (outs[key], n)
            if key[1]:
                got = swap(outs[key], order[key[0]][0], owners)
                for n, b in enumerate(outs_of[key]):
                    back[key[0], b ^ 1] = (got, n)
        return signals

    made = {}
    back = {}

    ahead = (1, 2, 3)
    signals = [
        stage("work_near", 0, [(q, 0, p) for p in ahead for q in (0, 1)]),
        stage("work_far", 1, [(q, f, p) for f in (1, 3) for p in ahead for q in (0, 1)]),
        stage("work_last", 2, [(q, 2, p) for p in ahead for q in (0, 1)]),
        stage("work_kept", 3, [(q, f, 0) for f in (0, 1, 3, 2) for q in (0, 1)]),
    ]

    def terms(k, b):
        return [made[k, b], back[k, b]] + [(got, bits.index(b)) for got, bits in later[k] if b in bits]

    later = {k: [] for k in every}
    for step in (1, 2, 3):
        bit = 1 << step
        sent = [b for b in range(owners) if b & bit and not b & (bit - 1)]
        sums = merge([[terms(k, b) for b in sent] for k in every], f"merge_{step}")
        for k in every:
            got = swap(sums[k], order[k][step], owners)
            later[k].append((got, [b ^ bit for b in sent]))
    leaving = leave(place, [terms(k, 0) for k in every])
    returned = lax.all_to_all(leaving, "dp", split_axis=0, concat_axis=0, tiled=True)

    flat = [(pair, a) for pair in (0, 1) for a in range(5)]
    parts = []
    for r in range(owners):
        parts.append([])
        for pair in (0, 1):
            origin, signal, unit = where[pair, r]
            parts[r].append((tuple((flat.index(a), i) for a, i in origin), signal, unit))
    panel_grad = panel_sum(
        table,
        jnp.arange(owners, dtype=jnp.int32) ^ me,
        [arrays[pair][a] for pair, a in flat],
        signals,
        parts,
        panels.shape,
    )
    return home(returned, rank), panel_grad


def solution(mesh):
    placed = (
        P(("dp", "label"), None),
        P(("dp", "label")),
        P(("dp", "label"), None, None),
        P(("dp", "label"), None),
        P(("dp", "label"), None),
        P(("dp", "label"), None),
    )
    return jax.shard_map(
        shards,
        mesh=mesh,
        in_specs=placed,
        out_specs=(P(("dp", "label"), None), P(("dp", "label"), None, None)),
        check_vma=False,
    )
```

```python
import functools
import jax
import jax.numpy as jnp
import numpy as np
from jax import lax
from jax.experimental import pallas as pl
from jax.experimental.pallas import tpu as pltpu
from jax.sharding import PartitionSpec as P

CAP = 2
CODE = 16
LIMIT = 63 << 20
BF = jnp.bfloat16
F32 = jnp.float32


def iota(shape, axis):
    return lax.broadcasted_iota(jnp.int32, shape, axis)


def dot(a, b, dims):
    return lax.dot_general(a, b, (dims, ((), ())), preferred_element_type=F32)


NN = ((1,), (0,))
NT = ((1,), (1,))
TN = ((0,), (0,))


def params(limit):
    return pltpu.CompilerParams(vmem_limit_bytes=limit)


def pack_body(groups, slots, x_ref, dest_ref, out_ref, rank_ref):
    rows = x_ref.shape[0]
    dest = dest_ref[...]
    target = dest // rows
    place = dest % rows
    member = jnp.where(iota((16, rows), 0) == target, 1.0, 0.0)
    earlier = jnp.where(iota((rows, rows), 0) < iota((rows, rows), 1), 1.0, 0.0).astype(BF)
    rank = jnp.sum(dot(member.astype(BF), earlier, NN) * member, axis=0, keepdims=True)
    rank = rank.astype(jnp.int32)
    rank_ref[...] = rank + target * slots
    kind = iota((CODE, rows), 0)
    code = jnp.where(kind == 0, place // 16, jnp.where(kind == 1, place % 16, 1))
    code = code.astype(F32).astype(BF)
    out_ref[:, slots:, :] = jnp.zeros((groups, CODE, x_ref.shape[1]), BF)
    for t in range(groups):
        pick = jnp.where(iota((slots, rows), 0) == jnp.where(target == t, rank, -1), 1.0, 0.0).astype(BF)
        out_ref[t, :slots, :] = dot(pick, x_ref[...], NN).astype(BF)
        out_ref[t, slots:, :slots] = dot(code, pick, NT).astype(BF)


def pack(x, dest, groups, slots):
    rows, width = x.shape
    return pl.pallas_call(
        functools.partial(pack_body, groups, slots),
        out_shape=(
            jax.ShapeDtypeStruct((groups, slots + CODE, width), BF),
            jax.ShapeDtypeStruct((1, rows), jnp.int32),
        ),
        compiler_params=params(LIMIT),
        name="pack_rows",
    )(x, dest)


def places(coded, slots):
    code = coded[:, :slots].astype(F32)
    place = (code[0:1] * 16.0 + code[1:2]).astype(jnp.int32)
    return jnp.where(code[2:3] > 0.5, place, -1)


def land_body(groups, slots, arrived_ref, code_ref, place_ref, *pair_refs):
    part = pair_refs[0].shape[1]
    rows = 2 * part * len(pair_refs)
    total = jnp.zeros((rows, arrived_ref.shape[2]), F32)
    for s in range(groups):
        place = places(arrived_ref[s, slots:, :], slots)
        place_ref[s : s + 1, :] = place
        put = jnp.where(iota((rows, slots), 0) == place, 1.0, 0.0).astype(BF)
        total += dot(put, arrived_ref[s, :slots, :], NN)
    for k in range(2 * len(pair_refs)):
        pair_refs[k // 2][k % 2] = total[k * part : (k + 1) * part].astype(BF)


def land(arrived, codes, rows, slots):
    groups, _, width = arrived.shape
    pair = jax.ShapeDtypeStruct((2, rows // STREAMS, width), BF)
    return pl.pallas_call(
        functools.partial(land_body, groups, slots),
        in_specs=[pl.BlockSpec(memory_space=pltpu.VMEM), pl.BlockSpec(memory_space=pltpu.HBM)],
        out_shape=(jax.ShapeDtypeStruct((groups, slots), jnp.int32), pair, pair),
        compiler_params=params(LIMIT),
        name="land_rows",
    )(arrived, codes)


def leave_body(groups, slots, terms, *refs):
    place_ref, out_ref = refs[0], refs[-1]
    streams = []
    for k in range(STREAMS):
        total = refs[1 + k * terms][0].astype(F32)
        for ref in refs[2 + k * terms : 1 + (k + 1) * terms]:
            total += ref[0].astype(F32)
        streams.append(total.astype(BF))
    grad = jnp.concatenate(streams, axis=0)
    rows = grad.shape[0]
    for s in range(groups):
        put = jnp.where(iota((rows, slots), 0) == place_ref[s : s + 1, :], 1.0, 0.0).astype(BF)
        out_ref[s] = dot(put, grad, TN).astype(BF)


def one_block(array, index, part):
    _, rows, width = array.shape
    return pl.BlockSpec((1, part, width), lambda i: (index, i, 0))


def leave(place, terms):
    groups, slots = place.shape
    flat = [term for stream in terms for term in stream]
    width = flat[0][0].shape[2]
    return pl.pallas_call(
        functools.partial(leave_body, groups, slots, len(terms[0])),
        grid=(1,),
        in_specs=[pl.BlockSpec((groups, slots), lambda i: (0, 0))]
        + [one_block(a, index, a.shape[1]) for a, index in flat],
        out_specs=pl.BlockSpec((groups, slots, width), lambda i: (0, 0, 0)),
        out_shape=jax.ShapeDtypeStruct((groups, slots, width), BF),
        compiler_params=params(LIMIT),
        name="leave_rows",
    )(place, *[a for a, _ in flat])


def merge_body(sums, *refs):
    outs = refs[-STREAMS:]
    at = 0
    for k, blocks in enumerate(sums):
        for j, terms in enumerate(blocks):
            total = refs[at][0].astype(F32)
            for ref in refs[at + 1 : at + len(terms)]:
                total += ref[0].astype(F32)
            outs[k][j] = total.astype(BF)
            at += len(terms)


def merge(sums, name):
    flat = [term for blocks in sums for terms in blocks for term in terms]
    _, rows, width = flat[0][0].shape
    count = len(sums[0])
    steps = 2
    part = rows // steps
    return pl.pallas_call(
        functools.partial(merge_body, [[[0] * len(t) for t in b] for b in sums]),
        grid=(steps,),
        in_specs=[one_block(a, index, part) for a, index in flat],
        out_specs=[pl.BlockSpec((count, part, width), lambda i: (0, i, 0))] * STREAMS,
        out_shape=[jax.ShapeDtypeStruct((count, rows, width), BF)] * STREAMS,
        compiler_params=params(LIMIT),
        cost_estimate=pl.CostEstimate(
            flops=0, transcendentals=0, bytes_accessed=2 * rows * width * (len(flat) + count * STREAMS)
        ),
        name=name,
    )(*[a for a, _ in flat])


def home_body(groups, slots, back_ref, rank_ref, out_ref):
    rows = out_ref.shape[0]
    total = jnp.zeros(out_ref.shape, F32)
    for t in range(groups):
        pick = jnp.where(iota((slots, rows), 0) + t * slots == rank_ref[...], 1.0, 0.0).astype(BF)
        total += dot(pick, back_ref[t], TN)
    out_ref[...] = total.astype(BF)


def home(back, rank):
    groups, slots, width = back.shape
    return pl.pallas_call(
        functools.partial(home_body, groups, slots),
        out_shape=jax.ShapeDtypeStruct((rank.shape[1], width), BF),
        compiler_params=params(LIMIT),
        name="home_rows",
    )(back, rank)


def cut_body(halves, *refs):
    n = len(halves)
    buf, in_sem, out_sem = refs[2 * n :]
    loads = [pltpu.make_async_copy(refs[i].at[h], buf.at[i], in_sem.at[i]) for i, h in enumerate(halves)]
    stores = [pltpu.make_async_copy(buf.at[i], refs[n + i], out_sem.at[i]) for i in range(n)]
    for load in loads:
        load.start()
    for load, store in zip(loads, stores):
        load.wait()
        store.start()
    for store in stores:
        store.wait()


def cut(items):
    n = len(items)
    loose = pl.BlockSpec(memory_space=pltpu.HBM)
    return pl.pallas_call(
        functools.partial(cut_body, [h for _, h in items]),
        in_specs=[loose] * n,
        out_specs=[loose] * n,
        out_shape=[jax.ShapeDtypeStruct(a.shape[1:], a.dtype) for a, _ in items],
        scratch_shapes=[
            pltpu.VMEM((n, *items[0][0].shape[1:]), items[0][0].dtype),
            pltpu.SemaphoreType.DMA((n,)),
            pltpu.SemaphoreType.DMA((n,)),
        ],
        compiler_params=params(LIMIT),
        name="cut_halves",
    )(*[a for a, _ in items])


def work_body(units, n_in, n_out, *refs):
    table_ref, meta_ref, code_hbm, w_hbm, scale_hbm = refs[:5]
    x_refs = refs[5 : 5 + n_in]
    out_refs = refs[5 + n_in : 5 + n_in + n_out]
    signal_ref = refs[5 + n_in + n_out]
    scratch = refs[6 + n_in + n_out :]
    x_buf, out_buf, signal_buf, w_ref, code_ref, lane_scale_ref, state_ref, in_sem, out_sem, signal_sem, w_sem, code_sem = (
        scratch
    )
    total = len(units)
    count, lanes, width = w_ref.shape
    rows = x_buf.shape[1]
    part = rows // 2

    def store(u):
        copies = [pltpu.make_async_copy(signal_buf.at[u], signal_ref.at[u], signal_sem.at[u])]
        for h, (array, block) in enumerate(units[u][1]):
            cut = out_buf.at[u, pl.ds(h * part, part)]
            copies.append(pltpu.make_async_copy(cut, out_refs[array].at[block], out_sem.at[2 * u + h]))
        return copies

    def fetch(u):
        for h, (array, index) in enumerate(units[u][0]):
            cut = x_buf.at[u, pl.ds(h * part, part)]
            pltpu.make_async_copy(x_refs[array].at[index], cut, in_sem.at[u]).start()

    def panel_copies(p):
        return (
            pltpu.make_async_copy(w_hbm.at[p], w_ref.at[p], w_sem.at[p, 0]),
            pltpu.make_async_copy(scale_hbm.at[p], lane_scale_ref.at[p], w_sem.at[p, 1]),
        )

    def ask(panel):
        @pl.when(state_ref[panel] == 0)
        def _():
            state_ref[panel] = 1
            for copy in panel_copies(panel):
                copy.start()

    def need(panel):
        @pl.when(state_ref[panel] == 1)
        def _():
            state_ref[panel] = 2
            for copy in panel_copies(panel):
                copy.wait()

    def slots_of(u):
        batch = meta_ref[0, u]
        first = table_ref[batch, 1]
        second = table_ref[batch, 3]
        use_first = jnp.maximum(first, 0)
        use_second = jnp.where(second >= 0, second, use_first)
        return batch, (first, second), (use_first, use_second)

    code_cut = code_hbm.at[:, pl.ds(0, 2)]
    code_copy = pltpu.make_async_copy(code_cut, code_ref, code_sem.at[0])
    code_copy.start()
    for p in range(count):
        state_ref[p] = 0
    for u in range(total):
        fetch(u)
        for panel in slots_of(u)[2]:
            ask(panel)
    code_copy.wait()

    def ready(u):
        pltpu.make_async_copy(x_buf.at[u], x_buf.at[u], in_sem.at[u]).wait()
        for panel in slots_of(u)[2]:
            need(panel)

    def signals(u):
        batch, asked, use = slots_of(u)
        code = code_ref[batch, meta_ref[1, u]].astype(F32).astype(jnp.int32)
        scores = dot(jnp.concatenate([w_ref[use[0]], w_ref[use[1]]], axis=0), x_buf[u], NT)
        for c in range(CAP):
            slot = table_ref[batch, 2 * c]
            weight = jnp.where(asked[c] >= 0, 1.0, 0.0)
            scale = jnp.concatenate([lane_scale_ref[use[c]].astype(F32)] * (rows // 128), axis=1)
            score = scores[c * lanes : (c + 1) * lanes] * scale
            lane = iota((lanes, rows), 0)
            hit = lane == jnp.where(code[0:1] == slot, code[4:5], -1)
            for k in range(1, 4):
                hit |= lane == jnp.where(code[k : k + 1] == slot, code[4 + k : 5 + k], -1)
            signal = (jax.nn.sigmoid(score) - jnp.where(hit, 1.0, 0.0)) * (scale * weight)
            signal_buf[u, c] = signal.astype(BF)

    def partial(u):
        use = slots_of(u)[2]
        total_grad = dot(signal_buf[u, 0], w_ref[use[0]], TN) + dot(signal_buf[u, 1], w_ref[use[1]], TN)
        out_buf[u] = total_grad.astype(BF)

    def send(u):
        for v in range(total):

            @pl.when(u == v)
            def _():
                for copy in store(v):
                    copy.start()

    ready(0)
    signals(0)

    def step(u, carry):
        ready(u)
        partial(u - 1)
        signals(u)
        send(u - 1)
        return carry

    lax.fori_loop(1, total, step, 0)
    partial(total - 1)
    for copy in store(total - 1):
        copy.start()
    for u in range(total):
        for copy in store(u):
            copy.wait()


def work(table, offsets, codes, panels, scales, arrays, units, out_blocks, name):
    count, lanes, width = panels.shape
    part = arrays[0].shape[-2]
    rows = 2 * part
    meta = np.array([offsets, [u[2] for u in units]], np.int32)
    total = len(units)
    scalar = pl.BlockSpec(memory_space=pltpu.SMEM)
    loose = pl.BlockSpec(memory_space=pltpu.HBM)
    outs = pl.pallas_call(
        functools.partial(work_body, units, len(arrays), len(out_blocks)),
        in_specs=[scalar, scalar, loose, loose, loose] + [loose] * len(arrays),
        out_specs=[loose] * len(out_blocks) + [loose],
        out_shape=[jax.ShapeDtypeStruct((n, part, width), BF) for n in out_blocks]
        + [jax.ShapeDtypeStruct((total, CAP, lanes, rows), BF)],
        scratch_shapes=[
            pltpu.VMEM((total, rows, width), BF),
            pltpu.VMEM((total, rows, width), BF),
            pltpu.VMEM((total, CAP, lanes, rows), BF),
            pltpu.VMEM(panels.shape, BF),
            pltpu.VMEM((codes.shape[0], 2, CODE, rows), BF),
            pltpu.VMEM(scales.shape, BF),
            pltpu.SMEM((count,), jnp.int32),
            pltpu.SemaphoreType.DMA((total,)),
            pltpu.SemaphoreType.DMA((2 * total,)),
            pltpu.SemaphoreType.DMA((total,)),
            pltpu.SemaphoreType.DMA((count, 2)),
            pltpu.SemaphoreType.DMA((1,)),
        ],
        compiler_params=params(LIMIT),
        cost_estimate=pl.CostEstimate(
            flops=total * 3 * lanes * rows * width * 4,
            transcendentals=0,
            bytes_accessed=panels.size * 2 + total * rows * (width * 4 + lanes * 2),
        ),
        name=name,
    )(table, meta, codes, panels, scales, *arrays)
    return outs[:-1], outs[-1]


def panel_body(parts, n_arrays, n_signals, *refs):
    table_ref = refs[0]
    x_refs = refs[1 : 1 + n_arrays]
    s_refs = refs[1 + n_arrays : 1 + n_arrays + n_signals]
    grad_ref, x_all, s_all, total_ref, x_sem, s_sem = refs[1 + n_arrays + n_signals :]
    rows = x_all.shape[1] // STREAMS
    for rel, pieces in enumerate(parts):
        for pair, (sources, signal, unit) in enumerate(pieces):
            wide = pl.ds(2 * pair * rows, 2 * rows)
            for h, (array, index) in enumerate(sources):
                cut = pl.ds((2 * pair + h) * rows, rows)
                pltpu.make_async_copy(x_refs[array].at[index], x_all.at[rel, cut], x_sem.at[rel]).start()
            pltpu.make_async_copy(s_refs[signal].at[unit], s_all.at[rel, :, :, wide], s_sem.at[rel]).start()
    total_ref[...] = jnp.zeros(total_ref.shape, F32)

    def batch(rel, carry):
        pltpu.make_async_copy(x_all.at[rel], x_all.at[rel], x_sem.at[rel]).wait()
        pltpu.make_async_copy(s_all.at[rel], s_all.at[rel], s_sem.at[rel]).wait()
        first = table_ref[rel, 1]
        second = table_ref[rel, 3]
        lanes = s_all.shape[2]

        @pl.when((first >= 0) & (second < 0))
        def _():
            total_ref[first] += dot(s_all[rel, 0], x_all[rel], NN)

        @pl.when(second >= 0)
        def _():
            both = dot(jnp.concatenate([s_all[rel, 0], s_all[rel, 1]], axis=0), x_all[rel], NN)
            total_ref[first] += both[:lanes]
            total_ref[second] += both[lanes:]

        return carry

    lax.fori_loop(0, len(parts), batch, 0)
    grad_ref[...] = total_ref[...].astype(BF)


def panel_sum(table, arrays, signals, parts, shape):
    count, lanes, width = shape
    rows = arrays[0].shape[2] * STREAMS
    scalar = pl.BlockSpec(memory_space=pltpu.SMEM)
    loose = pl.BlockSpec(memory_space=pltpu.HBM)
    return pl.pallas_call(
        functools.partial(panel_body, parts, len(arrays), len(signals)),
        in_specs=[scalar] + [loose] * (len(arrays) + len(signals)),
        out_specs=pl.BlockSpec(memory_space=pltpu.VMEM),
        out_shape=jax.ShapeDtypeStruct(shape, BF),
        scratch_shapes=[
            pltpu.VMEM((len(parts), rows, width), BF),
            pltpu.VMEM((len(parts), CAP, lanes, rows), BF),
            pltpu.VMEM(shape, F32),
            pltpu.SemaphoreType.DMA((len(parts),)),
            pltpu.SemaphoreType.DMA((len(parts),)),
        ],
        compiler_params=params(LIMIT),
        cost_estimate=pl.CostEstimate(
            flops=len(parts) * CAP * lanes * rows * width * 2,
            transcendentals=0,
            bytes_accessed=len(parts) * rows * (width + CAP * lanes) * 2 + count * lanes * width * 2,
        ),
        name="panel_grad",
    )(table, *arrays, *signals)


ORDERS = ((1, 3, 4, 12), (3, 1, 12, 4), (4, 12, 1, 3), (12, 4, 3, 1))
STREAMS = len(ORDERS)
RINGS = ((1, 3), (4, 12))


def swap(array, mask, owners):
    return lax.ppermute(array, "label", [(i, i ^ mask) for i in range(owners)])


def shards(queries, cluster_dest, panels, scales, shortlist, positives):
    rows, width = queries.shape
    count, lanes = scales.shape
    groups = lax.axis_size("dp")
    owners = lax.axis_size("label")
    slots = 3 * rows // (2 * groups)
    part = rows // STREAMS
    me = lax.axis_index("label").astype(jnp.int32)

    outgoing, rank = pack(queries, cluster_dest.reshape(1, rows), groups, slots)

    marks = jnp.transpose(positives.reshape(2, 2 * part, -1), (0, 2, 1))
    code = jnp.concatenate([marks // lanes, marks % lanes], axis=1).astype(F32).astype(BF)
    code = jnp.pad(code, ((0, 0), (0, CODE - code.shape[1]), (0, 0)))
    listed = jnp.pad(shortlist.astype(F32).astype(BF), ((0, CODE - 1), (0, 2 * part - shortlist.shape[1])))
    code = jnp.concatenate([code, listed[None]], axis=0)[None]
    outgoing, codes = lax.optimization_barrier((outgoing, code))
    arrived = lax.all_to_all(outgoing, "dp", split_axis=0, concat_axis=0, tiled=True)
    for step in range(4):
        codes = jnp.concatenate([codes, swap(codes, 1 << step, owners)], axis=0)
    place, *own = land(arrived, codes, rows, slots)
    wanted = codes[:, 2, 0, : shortlist.shape[1]].astype(F32).astype(jnp.int32)

    slot_ids = jnp.arange(wanted.shape[1], dtype=jnp.int32)[None, :]
    mine = wanted // count == me
    local = wanted % count
    first = jnp.min(jnp.where(mine, slot_ids, wanted.shape[1]), axis=1, keepdims=True)
    last = jnp.max(jnp.where(mine, slot_ids, -1), axis=1, keepdims=True)
    first_panel = jnp.max(jnp.where(slot_ids == first, local, -1), axis=1, keepdims=True)
    last_panel = jnp.max(jnp.where(slot_ids == last, local, -1), axis=1, keepdims=True)
    none = first_panel < 0
    single = none | (last == first)
    table = jnp.concatenate(
        [
            jnp.where(none, -1, first),
            first_panel,
            jnp.where(single, -1, last),
            jnp.where(single, -1, last_panel),
        ],
        axis=1,
    )

    every = range(STREAMS)
    order = ORDERS
    arrays = []
    for pair, (one, three) in zip(own, RINGS):
        by1, by3 = swap(pair, one, owners), swap(pair, three, owners)
        low, high = swap(by1[0], three, owners), swap(by3[1], one, owners)
        near = jnp.stack([pair, by1, jnp.stack([low, high]), by3], axis=1)
        arrays.append([near])

    for group, (one, three) in zip(arrays, RINGS[::-1]):
        group += [swap(group[0], one, owners), swap(group[0], three, owners)]
    halves = cut([(group[1 + h], h) for group in arrays for h in (0, 1)])
    for group, (one, three), (low, high) in zip(arrays, RINGS[::-1], (halves[:2], halves[2:])):
        group += [swap(low, three, owners), swap(high, one, owners)]

    def rel(k, bits):
        out = 0
        for s in range(4):
            if bits >> s & 1:
                out ^= order[k][s]
        return out

    where = {}
    wide_scales = jnp.broadcast_to(scales[:, :, None], (count, lanes, 128))

    def bits_of(k, r):
        return next(b for b in range(owners) if rel(k, b) == r)

    def stage(name, index, members):
        outs_of, units, ids, used = {}, [], [], []

        def source(array):
            if array not in used:
                used.append(array)
            return used.index(array)

        for pair, far, spot in members:
            r = 4 * far + spot if pair == 0 else 4 * spot + far
            legs = [(k, bits_of(k, r)) for k in (2 * pair, 2 * pair + 1)]
            if far == 2:
                origin = (((pair, 3), spot), ((pair, 4), spot))
            else:
                array = (pair, (0, 1, None, 2)[far])
                origin = ((array, (0, spot)), (array, (1, spot)))
            for k, b in legs:
                outs_of.setdefault((k, b & 1), []).append(b)
            where[pair, r] = (origin, index, len(units))
            units.append((tuple((source(a), i) for a, i in origin), legs, pair))
            ids.append(r)
        keys = sorted(outs_of)
        for key in keys:
            outs_of[key].sort(key=lambda b: (b >> 1 & 1, b))
        units = [
            (origin, tuple((keys.index((k, b & 1)), outs_of[k, b & 1].index(b)) for k, b in legs), pair)
            for origin, legs, pair in units
        ]
        blocks = [len(outs_of[key]) for key in keys]
        ins = [arrays[pair][a] for pair, a in used]
        outs, signals = work(table, ids, codes, panels, wide_scales, ins, units, blocks, name)
        outs = dict(zip(keys, outs))
        for key in keys:
            for n, b in enumerate(outs_of[key]):
                made[key[0], b] = (outs[key], n)
            if key[1]:
                got = swap(outs[key], order[key[0]][0], owners)
                for n, b in enumerate(outs_of[key]):
                    back[key[0], b ^ 1] = (got, n)
        return signals

    made = {}
    back = {}

    ahead = (1, 2, 3)
    signals = [
        stage("work_near", 0, [(q, 0, p) for p in ahead for q in (0, 1)]),
        stage("work_far", 1, [(q, f, p) for f in (1, 3) for p in ahead for q in (0, 1)]),
        stage("work_last", 2, [(q, 2, p) for p in ahead for q in (0, 1)]),
        stage("work_kept", 3, [(q, f, 0) for f in (0, 1, 3, 2) for q in (0, 1)]),
    ]

    def terms(k, b):
        return [made[k, b], back[k, b]] + [(got, bits.index(b)) for got, bits in later[k] if b in bits]

    later = {k: [] for k in every}
    for step in (1, 2, 3):
        bit = 1 << step
        sent = [b for b in range(owners) if b & bit and not b & (bit - 1)]
        sums = merge([[terms(k, b) for b in sent] for k in every], f"merge_{step}")
        for k in every:
            got = swap(sums[k], order[k][step], owners)
            later[k].append((got, [b ^ bit for b in sent]))
    leaving = leave(place, [terms(k, 0) for k in every])
    returned = lax.all_to_all(leaving, "dp", split_axis=0, concat_axis=0, tiled=True)

    flat = [(pair, a) for pair in (0, 1) for a in range(5)]
    parts = []
    for r in range(owners):
        parts.append([])
        for pair in (0, 1):
            origin, signal, unit = where[pair, r]
            parts[r].append((tuple((flat.index(a), i) for a, i in origin), signal, unit))
    panel_grad = panel_sum(
        table,
        [arrays[pair][a] for pair, a in flat],
        signals,
        parts,
        panels.shape,
    )
    return home(returned, rank), panel_grad


def solution(mesh):
    placed = (
        P(("dp", "label"), None),
        P(("dp", "label")),
        P(("dp", "label"), None, None),
        P(("dp", "label"), None),
        P(("dp", "label"), None),
        P(("dp", "label"), None),
    )
    return jax.shard_map(
        shards,
        mesh=mesh,
        in_specs=placed,
        out_specs=(P(("dp", "label"), None), P(("dp", "label"), None, None)),
        check_vma=False,
    )
```

```python
import functools
import jax
import jax.numpy as jnp
import numpy as np
from jax import lax
from jax.experimental import pallas as pl
from jax.experimental.pallas import tpu as pltpu
from jax.sharding import PartitionSpec as P

CAP = 2
CODE = 16
LIMIT = 63 << 20
BF = jnp.bfloat16
F32 = jnp.float32


def iota(shape, axis):
    return lax.broadcasted_iota(jnp.int32, shape, axis)


def dot(a, b, dims):
    return lax.dot_general(a, b, (dims, ((), ())), preferred_element_type=F32)


NN = ((1,), (0,))
NT = ((1,), (1,))
TN = ((0,), (0,))


def params(limit):
    return pltpu.CompilerParams(vmem_limit_bytes=limit)


def pack_body(groups, slots, x_ref, dest_ref, out_ref, rank_ref):
    rows = x_ref.shape[0]
    dest = dest_ref[...]
    target = dest // rows
    place = dest % rows
    member = jnp.where(iota((16, rows), 0) == target, 1.0, 0.0)
    earlier = jnp.where(iota((rows, rows), 0) < iota((rows, rows), 1), 1.0, 0.0).astype(BF)
    rank = jnp.sum(dot(member.astype(BF), earlier, NN) * member, axis=0, keepdims=True)
    rank = rank.astype(jnp.int32)
    rank_ref[...] = rank + target * slots
    kind = iota((CODE, rows), 0)
    code = jnp.where(kind == 0, place // 16, jnp.where(kind == 1, place % 16, 1))
    code = code.astype(F32).astype(BF)
    out_ref[:, slots:, :] = jnp.zeros((groups, CODE, x_ref.shape[1]), BF)
    for t in range(groups):
        pick = jnp.where(iota((slots, rows), 0) == jnp.where(target == t, rank, -1), 1.0, 0.0).astype(BF)
        out_ref[t, :slots, :] = dot(pick, x_ref[...], NN).astype(BF)
        out_ref[t, slots:, :slots] = dot(code, pick, NT).astype(BF)


def pack(x, dest, groups, slots):
    rows, width = x.shape
    return pl.pallas_call(
        functools.partial(pack_body, groups, slots),
        out_shape=(
            jax.ShapeDtypeStruct((groups, slots + CODE, width), BF),
            jax.ShapeDtypeStruct((1, rows), jnp.int32),
        ),
        compiler_params=params(LIMIT),
        name="pack_rows",
    )(x, dest)


def land_body(groups, slots, arrived_ref, code_ref, put_ref, *pair_refs):
    part = pair_refs[0].shape[1]
    rows = 2 * part * len(pair_refs)
    width = arrived_ref.shape[2]
    for s in range(groups):
        code = jnp.transpose(arrived_ref[s, slots:, :128].astype(F32))[:slots]
        place = jnp.where(code[:, 2:3] > 0.5, code[:, 0:1] * 16.0 + code[:, 1:2], -1.0).astype(jnp.int32)
        put = jnp.where(iota((slots, rows), 1) == place, 1.0, 0.0).astype(BF)
        put_ref[s * slots : (s + 1) * slots, :] = put
    sent = arrived_ref[:, :slots, :].reshape(groups * slots, width)
    total = dot(put_ref[...], sent, TN)
    for k in range(2 * len(pair_refs)):
        pair_refs[k // 2][k % 2] = total[k * part : (k + 1) * part].astype(BF)


def land(arrived, codes, rows, slots):
    groups, _, width = arrived.shape
    pair = jax.ShapeDtypeStruct((2, rows // STREAMS, width), BF)
    return pl.pallas_call(
        functools.partial(land_body, groups, slots),
        in_specs=[pl.BlockSpec(memory_space=pltpu.VMEM), pl.BlockSpec(memory_space=pltpu.HBM)],
        out_shape=(jax.ShapeDtypeStruct((groups * slots, rows), BF), pair, pair),
        compiler_params=params(LIMIT),
        name="land_rows",
    )(arrived, codes)


def leave_body(groups, slots, terms, *refs):
    put_ref, out_ref = refs[0], refs[-1]
    streams = []
    for k in range(STREAMS):
        total = refs[1 + k * terms][0].astype(F32)
        for ref in refs[2 + k * terms : 1 + (k + 1) * terms]:
            total += ref[0].astype(F32)
        streams.append(total.astype(BF))
    grad = jnp.concatenate(streams, axis=0)
    out_ref[...] = dot(put_ref[...], grad, NN).astype(BF).reshape(groups, slots, grad.shape[1])


def one_block(array, index, part):
    _, rows, width = array.shape
    return pl.BlockSpec((1, part, width), lambda i: (index, i, 0))


def leave(put, terms, groups):
    slots = put.shape[0] // groups
    flat = [term for stream in terms for term in stream]
    width = flat[0][0].shape[2]
    return pl.pallas_call(
        functools.partial(leave_body, groups, slots, len(terms[0])),
        grid=(1,),
        in_specs=[pl.BlockSpec(put.shape, lambda i: (0, 0))]
        + [one_block(a, index, a.shape[1]) for a, index in flat],
        out_specs=pl.BlockSpec((groups, slots, width), lambda i: (0, 0, 0)),
        out_shape=jax.ShapeDtypeStruct((groups, slots, width), BF),
        compiler_params=params(LIMIT),
        name="leave_rows",
    )(put, *[a for a, _ in flat])


def merge_body(sums, *refs):
    outs = refs[-STREAMS:]
    at = 0
    for k, blocks in enumerate(sums):
        for j, terms in enumerate(blocks):
            total = refs[at][0].astype(F32)
            for ref in refs[at + 1 : at + len(terms)]:
                total += ref[0].astype(F32)
            outs[k][j] = total.astype(BF)
            at += len(terms)


def merge(sums, name):
    flat = [term for blocks in sums for terms in blocks for term in terms]
    _, rows, width = flat[0][0].shape
    count = len(sums[0])
    steps = 2
    part = rows // steps
    return pl.pallas_call(
        functools.partial(merge_body, [[[0] * len(t) for t in b] for b in sums]),
        grid=(steps,),
        in_specs=[one_block(a, index, part) for a, index in flat],
        out_specs=[pl.BlockSpec((count, part, width), lambda i: (0, i, 0))] * STREAMS,
        out_shape=[jax.ShapeDtypeStruct((count, rows, width), BF)] * STREAMS,
        compiler_params=params(LIMIT),
        cost_estimate=pl.CostEstimate(
            flops=0, transcendentals=0, bytes_accessed=2 * rows * width * (len(flat) + count * STREAMS)
        ),
        name=name,
    )(*[a for a, _ in flat])


def home_body(groups, slots, back_ref, rank_ref, out_ref):
    rows, width = out_ref.shape
    pick = jnp.where(iota((groups * slots, rows), 0) == rank_ref[...], 1.0, 0.0).astype(BF)
    out_ref[...] = dot(pick, back_ref[...].reshape(groups * slots, width), TN).astype(BF)


def home(back, rank):
    groups, slots, width = back.shape
    return pl.pallas_call(
        functools.partial(home_body, groups, slots),
        out_shape=jax.ShapeDtypeStruct((rank.shape[1], width), BF),
        compiler_params=params(LIMIT),
        name="home_rows",
    )(back, rank)


def cut_body(halves, *refs):
    n = len(halves)
    buf, in_sem, out_sem = refs[2 * n :]
    loads = [pltpu.make_async_copy(refs[i].at[h], buf.at[i], in_sem.at[i]) for i, h in enumerate(halves)]
    stores = [pltpu.make_async_copy(buf.at[i], refs[n + i], out_sem.at[i]) for i in range(n)]
    for load in loads:
        load.start()
    for load, store in zip(loads, stores):
        load.wait()
        store.start()
    for store in stores:
        store.wait()


def cut(items):
    n = len(items)
    loose = pl.BlockSpec(memory_space=pltpu.HBM)
    return pl.pallas_call(
        functools.partial(cut_body, [h for _, h in items]),
        in_specs=[loose] * n,
        out_specs=[loose] * n,
        out_shape=[jax.ShapeDtypeStruct(a.shape[1:], a.dtype) for a, _ in items],
        scratch_shapes=[
            pltpu.VMEM((n, *items[0][0].shape[1:]), items[0][0].dtype),
            pltpu.SemaphoreType.DMA((n,)),
            pltpu.SemaphoreType.DMA((n,)),
        ],
        compiler_params=params(LIMIT),
        name="cut_halves",
    )(*[a for a, _ in items])


def work_body(units, n_in, n_out, *refs):
    table_ref, meta_ref, code_hbm, w_hbm, scale_hbm = refs[:5]
    x_refs = refs[5 : 5 + n_in]
    out_refs = refs[5 + n_in : 5 + n_in + n_out]
    signal_ref = refs[5 + n_in + n_out]
    scratch = refs[6 + n_in + n_out :]
    x_buf, out_buf, signal_buf, w_ref, code_ref, lane_scale_ref, state_ref, in_sem, out_sem, signal_sem, w_sem, code_sem = (
        scratch
    )
    total = len(units)
    count, lanes, width = w_ref.shape
    rows = x_buf.shape[1]
    part = rows // 2

    def store(u):
        copies = [pltpu.make_async_copy(signal_buf.at[u], signal_ref.at[u], signal_sem.at[u])]
        for h, (array, block) in enumerate(units[u][1]):
            cut = out_buf.at[u, pl.ds(h * part, part)]
            copies.append(pltpu.make_async_copy(cut, out_refs[array].at[block], out_sem.at[2 * u + h]))
        return copies

    def fetch(u):
        for h, (array, index) in enumerate(units[u][0]):
            cut = x_buf.at[u, pl.ds(h * part, part)]
            pltpu.make_async_copy(x_refs[array].at[index], cut, in_sem.at[u]).start()

    def panel_copies(p):
        return (
            pltpu.make_async_copy(w_hbm.at[p], w_ref.at[p], w_sem.at[p, 0]),
            pltpu.make_async_copy(scale_hbm.at[p], lane_scale_ref.at[p], w_sem.at[p, 1]),
        )

    def ask(panel):
        @pl.when(state_ref[panel] == 0)
        def _():
            state_ref[panel] = 1
            for copy in panel_copies(panel):
                copy.start()

    def need(panel):
        @pl.when(state_ref[panel] == 1)
        def _():
            state_ref[panel] = 2
            for copy in panel_copies(panel):
                copy.wait()

    def slots_of(u):
        batch = meta_ref[0, u]
        first = table_ref[batch, 1]
        second = table_ref[batch, 3]
        use_first = jnp.maximum(first, 0)
        use_second = jnp.where(second >= 0, second, use_first)
        return batch, (first, second), (use_first, use_second)

    code_cut = code_hbm.at[:, 0]
    code_copy = pltpu.make_async_copy(code_cut, code_ref, code_sem.at[0])
    code_copy.start()
    for p in range(count):
        state_ref[p] = 0
    for u in range(total):
        fetch(u)
        for panel in slots_of(u)[2]:
            ask(panel)
    code_copy.wait()

    def ready(u):
        pltpu.make_async_copy(x_buf.at[u], x_buf.at[u], in_sem.at[u]).wait()
        for panel in slots_of(u)[2]:
            need(panel)

    def signals(u):
        batch, asked, use = slots_of(u)
        code = code_ref[batch].astype(F32).astype(jnp.int32)
        code = jnp.where(meta_ref[1, u] == 0, code[: CODE // 2], code[CODE // 2 :])
        scores = dot(jnp.concatenate([w_ref[use[0]], w_ref[use[1]]], axis=0), x_buf[u], NT)
        for c in range(CAP):
            slot = table_ref[batch, 2 * c]
            weight = jnp.where(asked[c] >= 0, 1.0, 0.0)
            scale = jnp.concatenate([lane_scale_ref[use[c]].astype(F32)] * (rows // 128), axis=1)
            score = scores[c * lanes : (c + 1) * lanes] * scale
            lane = iota((lanes, rows), 0)
            hit = lane == jnp.where(code[0:1] == slot, code[4:5], -1)
            for k in range(1, 4):
                hit |= lane == jnp.where(code[k : k + 1] == slot, code[4 + k : 5 + k], -1)
            signal = (jax.nn.sigmoid(score) - jnp.where(hit, 1.0, 0.0)) * (scale * weight)
            signal_buf[u, c] = signal.astype(BF)

    def partial(u):
        use = slots_of(u)[2]
        total_grad = dot(signal_buf[u, 0], w_ref[use[0]], TN) + dot(signal_buf[u, 1], w_ref[use[1]], TN)
        out_buf[u] = total_grad.astype(BF)

    def send(u):
        for v in range(total):

            @pl.when(u == v)
            def _():
                for copy in store(v):
                    copy.start()

    ready(0)
    signals(0)

    def step(u, carry):
        ready(u)
        partial(u - 1)
        signals(u)
        send(u - 1)
        return carry

    lax.fori_loop(1, total, step, 0)
    partial(total - 1)
    for copy in store(total - 1):
        copy.start()
    for u in range(total):
        for copy in store(u):
            copy.wait()


def work(table, offsets, codes, panels, scales, arrays, units, out_blocks, name):
    count, lanes, width = panels.shape
    part = arrays[0].shape[-2]
    rows = 2 * part
    meta = np.array([offsets, [u[2] for u in units]], np.int32)
    total = len(units)
    scalar = pl.BlockSpec(memory_space=pltpu.SMEM)
    loose = pl.BlockSpec(memory_space=pltpu.HBM)
    outs = pl.pallas_call(
        functools.partial(work_body, units, len(arrays), len(out_blocks)),
        in_specs=[scalar, scalar, loose, loose, loose] + [loose] * len(arrays),
        out_specs=[loose] * len(out_blocks) + [loose],
        out_shape=[jax.ShapeDtypeStruct((n, part, width), BF) for n in out_blocks]
        + [jax.ShapeDtypeStruct((total, CAP, lanes, rows), BF)],
        scratch_shapes=[
            pltpu.VMEM((total, rows, width), BF),
            pltpu.VMEM((total, rows, width), BF),
            pltpu.VMEM((total, CAP, lanes, rows), BF),
            pltpu.VMEM(panels.shape, BF),
            pltpu.VMEM((codes.shape[0], CODE, rows), BF),
            pltpu.VMEM(scales.shape, BF),
            pltpu.SMEM((count,), jnp.int32),
            pltpu.SemaphoreType.DMA((total,)),
            pltpu.SemaphoreType.DMA((2 * total,)),
            pltpu.SemaphoreType.DMA((total,)),
            pltpu.SemaphoreType.DMA((count, 2)),
            pltpu.SemaphoreType.DMA((1,)),
        ],
        compiler_params=params(LIMIT),
        cost_estimate=pl.CostEstimate(
            flops=total * 3 * lanes * rows * width * 4,
            transcendentals=0,
            bytes_accessed=panels.size * 2 + total * rows * (width * 4 + lanes * 2),
        ),
        name=name,
    )(table, meta, codes, panels, scales, *arrays)
    return outs[:-1], outs[-1]


def panel_body(parts, n_arrays, n_signals, *refs):
    table_ref = refs[0]
    x_refs = refs[1 : 1 + n_arrays]
    s_refs = refs[1 + n_arrays : 1 + n_arrays + n_signals]
    grad_ref, x_all, s_all, total_ref, x_sem, s_sem = refs[1 + n_arrays + n_signals :]
    rows = x_all.shape[1] // STREAMS
    for rel, pieces in enumerate(parts):
        for pair, (sources, signal, unit) in enumerate(pieces):
            wide = pl.ds(2 * pair * rows, 2 * rows)
            for h, (array, index) in enumerate(sources):
                cut = pl.ds((2 * pair + h) * rows, rows)
                pltpu.make_async_copy(x_refs[array].at[index], x_all.at[rel, cut], x_sem.at[rel]).start()
            pltpu.make_async_copy(s_refs[signal].at[unit], s_all.at[rel, :, :, wide], s_sem.at[rel]).start()
    total_ref[...] = jnp.zeros(total_ref.shape, F32)

    def batch(rel, carry):
        pltpu.make_async_copy(x_all.at[rel], x_all.at[rel], x_sem.at[rel]).wait()
        pltpu.make_async_copy(s_all.at[rel], s_all.at[rel], s_sem.at[rel]).wait()
        first = table_ref[rel, 1]
        second = table_ref[rel, 3]
        lanes = s_all.shape[2]

        @pl.when((first >= 0) & (second < 0))
        def _():
            total_ref[first] += dot(s_all[rel, 0], x_all[rel], NN)

        @pl.when(second >= 0)
        def _():
            both = dot(jnp.concatenate([s_all[rel, 0], s_all[rel, 1]], axis=0), x_all[rel], NN)
            total_ref[first] += both[:lanes]
            total_ref[second] += both[lanes:]

        return carry

    lax.fori_loop(0, len(parts), batch, 0)
    grad_ref[...] = total_ref[...].astype(BF)


def panel_sum(table, arrays, signals, parts, shape):
    count, lanes, width = shape
    rows = arrays[0].shape[2] * STREAMS
    scalar = pl.BlockSpec(memory_space=pltpu.SMEM)
    loose = pl.BlockSpec(memory_space=pltpu.HBM)
    return pl.pallas_call(
        functools.partial(panel_body, parts, len(arrays), len(signals)),
        in_specs=[scalar] + [loose] * (len(arrays) + len(signals)),
        out_specs=pl.BlockSpec(memory_space=pltpu.VMEM),
        out_shape=jax.ShapeDtypeStruct(shape, BF),
        scratch_shapes=[
            pltpu.VMEM((len(parts), rows, width), BF),
            pltpu.VMEM((len(parts), CAP, lanes, rows), BF),
            pltpu.VMEM(shape, F32),
            pltpu.SemaphoreType.DMA((len(parts),)),
            pltpu.SemaphoreType.DMA((len(parts),)),
        ],
        compiler_params=params(LIMIT),
        cost_estimate=pl.CostEstimate(
            flops=len(parts) * CAP * lanes * rows * width * 2,
            transcendentals=0,
            bytes_accessed=len(parts) * rows * (width + CAP * lanes) * 2 + count * lanes * width * 2,
        ),
        name="panel_grad",
    )(table, *arrays, *signals)


ORDERS = ((1, 3, 4, 12), (3, 1, 12, 4), (4, 12, 1, 3), (12, 4, 3, 1))
STREAMS = len(ORDERS)
RINGS = ((1, 3), (4, 12))
SPREAD = [0]
for mask in ORDERS[0]:
    SPREAD += [r ^ mask for r in SPREAD]


def swap(array, mask, owners):
    return lax.ppermute(array, "label", [(i, i ^ mask) for i in range(owners)])


def shards(queries, cluster_dest, panels, scales, shortlist, positives):
    rows, width = queries.shape
    count, lanes = scales.shape
    groups = lax.axis_size("dp")
    owners = lax.axis_size("label")
    slots = 3 * rows // (2 * groups)
    part = rows // STREAMS
    every = range(STREAMS)
    order = ORDERS
    me = lax.axis_index("label").astype(jnp.int32)

    outgoing, rank = pack(queries, cluster_dest.reshape(1, rows), groups, slots)

    marks = jnp.transpose(positives.reshape(2, 2 * part, -1), (0, 2, 1))
    code = jnp.concatenate([marks // lanes, marks % lanes], axis=1).reshape(CODE, 2 * part)
    listed = jnp.pad(shortlist, ((0, CODE - 1), (0, 2 * part - shortlist.shape[1])))
    code = jnp.stack([code, listed]).astype(F32).astype(BF)[None]
    outgoing, codes = lax.optimization_barrier((outgoing, code))
    arrived = lax.all_to_all(outgoing, "dp", split_axis=0, concat_axis=0, tiled=True)
    for mask in order[0]:
        codes = jnp.concatenate([codes, swap(codes, mask, owners)], axis=0)
    put, *own = land(arrived, codes, rows, slots)
    wanted = codes[:, 1, 0, : shortlist.shape[1]].astype(F32).astype(jnp.int32)

    slot_ids = jnp.arange(wanted.shape[1], dtype=jnp.int32)[None, :]
    mine = wanted // count == me
    local = wanted % count
    first = jnp.min(jnp.where(mine, slot_ids, wanted.shape[1]), axis=1, keepdims=True)
    last = jnp.max(jnp.where(mine, slot_ids, -1), axis=1, keepdims=True)
    first_panel = jnp.max(jnp.where(slot_ids == first, local, -1), axis=1, keepdims=True)
    last_panel = jnp.max(jnp.where(slot_ids == last, local, -1), axis=1, keepdims=True)
    none = first_panel < 0
    single = none | (last == first)
    table = jnp.concatenate(
        [
            jnp.where(none, -1, first),
            first_panel,
            jnp.where(single, -1, last),
            jnp.where(single, -1, last_panel),
        ],
        axis=1,
    )

    arrays = []
    for pair, (one, three) in zip(own, RINGS):
        by1, by3 = swap(pair, one, owners), swap(pair, three, owners)
        low, high = swap(by1[0], three, owners), swap(by3[1], one, owners)
        near = jnp.stack([pair, by1, jnp.stack([low, high]), by3], axis=1)
        arrays.append([near])

    for group, (one, three) in zip(arrays, RINGS[::-1]):
        group += [swap(group[0], one, owners), swap(group[0], three, owners)]
    halves = cut([(group[1 + h], h) for group in arrays for h in (0, 1)])
    for group, (one, three), (low, high) in zip(arrays, RINGS[::-1], (halves[:2], halves[2:])):
        group += [swap(low, three, owners), swap(high, one, owners)]

    def rel(k, bits):
        out = 0
        for s in range(4):
            if bits >> s & 1:
                out ^= order[k][s]
        return out

    where = {}
    wide_scales = jnp.broadcast_to(scales[:, :, None], (count, lanes, 128))

    def bits_of(k, r):
        return next(b for b in range(owners) if rel(k, b) == r)

    def stage(name, index, members):
        outs_of, units, ids, used = {}, [], [], []

        def source(array):
            if array not in used:
                used.append(array)
            return used.index(array)

        for pair, far, spot in members:
            r = 4 * far + spot if pair == 0 else 4 * spot + far
            legs = [(k, bits_of(k, r)) for k in (2 * pair, 2 * pair + 1)]
            if far == 2:
                origin = (((pair, 3), spot), ((pair, 4), spot))
            else:
                array = (pair, (0, 1, None, 2)[far])
                origin = ((array, (0, spot)), (array, (1, spot)))
            for k, b in legs:
                outs_of.setdefault((k, b & 1), []).append(b)
            where[pair, r] = (origin, index, len(units))
            units.append((tuple((source(a), i) for a, i in origin), legs, pair))
            ids.append(SPREAD.index(r))
        keys = sorted(outs_of)
        for key in keys:
            outs_of[key].sort(key=lambda b: (b >> 1 & 1, b))
        units = [
            (origin, tuple((keys.index((k, b & 1)), outs_of[k, b & 1].index(b)) for k, b in legs), pair)
            for origin, legs, pair in units
        ]
        blocks = [len(outs_of[key]) for key in keys]
        ins = [arrays[pair][a] for pair, a in used]
        outs, signals = work(table, ids, codes, panels, wide_scales, ins, units, blocks, name)
        outs = dict(zip(keys, outs))
        for key in keys:
            for n, b in enumerate(outs_of[key]):
                made[key[0], b] = (outs[key], n)
            if key[1]:
                got = swap(outs[key], order[key[0]][0], owners)
                for n, b in enumerate(outs_of[key]):
                    back[key[0], b ^ 1] = (got, n)
        return signals

    made = {}
    back = {}

    ahead = (1, 2, 3)
    signals = [
        stage("work_near", 0, [(q, 0, p) for p in ahead for q in (0, 1)]),
        stage("work_far", 1, [(q, f, p) for f in (1, 3) for p in ahead for q in (0, 1)]),
        stage("work_last", 2, [(q, 2, p) for p in ahead for q in (0, 1)]),
        stage("work_kept", 3, [(q, f, 0) for f in (0, 1, 3, 2) for q in (0, 1)]),
    ]

    def terms(k, b):
        return [made[k, b], back[k, b]] + [(got, bits.index(b)) for got, bits in later[k] if b in bits]

    later = {k: [] for k in every}
    for step in (1, 2, 3):
        bit = 1 << step
        sent = [b for b in range(owners) if b & bit and not b & (bit - 1)]
        sums = merge([[terms(k, b) for b in sent] for k in every], f"merge_{step}")
        for k in every:
            later[k].append((swap(sums[k], order[k][step], owners), [b ^ bit for b in sent]))
    leaving = leave(put, [terms(k, 0) for k in every], groups)
    returned = lax.all_to_all(leaving, "dp", split_axis=0, concat_axis=0, tiled=True)

    flat = [(pair, a) for pair in (0, 1) for a in range(5)]
    parts = []
    for r in SPREAD:
        parts.append([])
        for pair in (0, 1):
            origin, signal, unit = where[pair, r]
            parts[-1].append((tuple((flat.index(a), i) for a, i in origin), signal, unit))
    panel_grad = panel_sum(
        table,
        [arrays[pair][a] for pair, a in flat],
        signals,
        parts,
        panels.shape,
    )
    return home(returned, rank), panel_grad


def solution(mesh):
    placed = (
        P(("dp", "label"), None),
        P(("dp", "label")),
        P(("dp", "label"), None, None),
        P(("dp", "label"), None),
        P(("dp", "label"), None),
        P(("dp", "label"), None),
    )
    return jax.shard_map(
        shards,
        mesh=mesh,
        in_specs=placed,
        out_specs=(P(("dp", "label"), None), P(("dp", "label"), None, None)),
        check_vma=False,
    )
```

```python
import functools
import jax
import jax.numpy as jnp
import numpy as np
from jax import lax
from jax.experimental import pallas as pl
from jax.experimental.pallas import tpu as pltpu
from jax.sharding import PartitionSpec as P

CAP = 2
CODE = 16
LIMIT = 63 << 20
BF = jnp.bfloat16
F32 = jnp.float32


def iota(shape, axis):
    return lax.broadcasted_iota(jnp.int32, shape, axis)


def dot(a, b, dims):
    return lax.dot_general(a, b, (dims, ((), ())), preferred_element_type=F32)


NN = ((1,), (0,))
NT = ((1,), (1,))
TN = ((0,), (0,))


def params(limit):
    return pltpu.CompilerParams(vmem_limit_bytes=limit)


def pack_body(groups, slots, x_ref, dest_ref, out_ref, rank_ref):
    rows = x_ref.shape[0]
    dest = dest_ref[...]
    target = dest // rows
    place = dest % rows
    member = jnp.where(iota((16, rows), 0) == target, 1.0, 0.0)
    earlier = jnp.where(iota((rows, rows), 0) < iota((rows, rows), 1), 1.0, 0.0).astype(BF)
    rank = jnp.sum(dot(member.astype(BF), earlier, NN) * member, axis=0, keepdims=True)
    rank = rank.astype(jnp.int32)
    rank_ref[...] = rank + target * slots
    kind = iota((CODE, rows), 0)
    code = jnp.where(kind == 0, place // 16, jnp.where(kind == 1, place % 16, 1))
    code = code.astype(F32).astype(BF)
    out_ref[:, slots:, :] = jnp.zeros((groups, CODE, x_ref.shape[1]), BF)
    for t in range(groups):
        pick = jnp.where(iota((slots, rows), 0) == jnp.where(target == t, rank, -1), 1.0, 0.0).astype(BF)
        out_ref[t, :slots, :] = dot(pick, x_ref[...], NN).astype(BF)
        out_ref[t, slots:, :slots] = dot(code, pick, NT).astype(BF)


def pack(x, dest, groups, slots):
    rows, width = x.shape
    return pl.pallas_call(
        functools.partial(pack_body, groups, slots),
        out_shape=(
            jax.ShapeDtypeStruct((groups, slots + CODE, width), BF),
            jax.ShapeDtypeStruct((1, rows), jnp.int32),
        ),
        compiler_params=params(LIMIT),
        name="pack_rows",
    )(x, dest)


def land_body(groups, slots, arrived_ref, code_ref, put_ref, *pair_refs):
    part = pair_refs[0].shape[1]
    rows = 2 * part * len(pair_refs)
    width = arrived_ref.shape[2]
    for s in range(groups):
        code = jnp.transpose(arrived_ref[s, slots:, :128].astype(F32))[:slots]
        place = jnp.where(code[:, 2:3] > 0.5, code[:, 0:1] * 16.0 + code[:, 1:2], -1.0).astype(jnp.int32)
        put = jnp.where(iota((slots, rows), 1) == place, 1.0, 0.0).astype(BF)
        put_ref[s * slots : (s + 1) * slots, :] = put
    sent = arrived_ref[:, :slots, :].reshape(groups * slots, width)
    total = dot(put_ref[...], sent, TN)
    for k in range(2 * len(pair_refs)):
        pair_refs[k // 2][k % 2] = total[k * part : (k + 1) * part].astype(BF)


def land(arrived, codes, rows, slots):
    groups, _, width = arrived.shape
    pair = jax.ShapeDtypeStruct((2, rows // STREAMS, width), BF)
    return pl.pallas_call(
        functools.partial(land_body, groups, slots),
        in_specs=[pl.BlockSpec(memory_space=pltpu.VMEM), pl.BlockSpec(memory_space=pltpu.HBM)],
        out_shape=(jax.ShapeDtypeStruct((groups * slots, rows), BF), pair, pair),
        compiler_params=params(LIMIT),
        name="land_rows",
    )(arrived, codes)


def leave_body(groups, slots, terms, *refs):
    put_ref, out_ref = refs[0], refs[-1]
    streams = []
    for k in range(STREAMS):
        total = refs[1 + k * terms][0].astype(F32)
        for ref in refs[2 + k * terms : 1 + (k + 1) * terms]:
            total += ref[0].astype(F32)
        streams.append(total.astype(BF))
    grad = jnp.concatenate(streams, axis=0)
    out_ref[...] = dot(put_ref[...], grad, NN).astype(BF).reshape(groups, slots, grad.shape[1])


def one_block(array, index, part):
    _, rows, width = array.shape
    return pl.BlockSpec((1, part, width), lambda i: (index, i, 0))


def leave(put, terms, groups):
    slots = put.shape[0] // groups
    flat = [term for stream in terms for term in stream]
    width = flat[0][0].shape[2]
    return pl.pallas_call(
        functools.partial(leave_body, groups, slots, len(terms[0])),
        grid=(1,),
        in_specs=[pl.BlockSpec(put.shape, lambda i: (0, 0))]
        + [one_block(a, index, a.shape[1]) for a, index in flat],
        out_specs=pl.BlockSpec((groups, slots, width), lambda i: (0, 0, 0)),
        out_shape=jax.ShapeDtypeStruct((groups, slots, width), BF),
        compiler_params=params(LIMIT),
        name="leave_rows",
    )(put, *[a for a, _ in flat])


def merge_body(sums, *refs):
    outs = refs[-STREAMS:]
    at = 0
    for k, blocks in enumerate(sums):
        for j, terms in enumerate(blocks):
            total = refs[at][0].astype(F32)
            for ref in refs[at + 1 : at + len(terms)]:
                total += ref[0].astype(F32)
            outs[k][j] = total.astype(BF)
            at += len(terms)


def merge(sums, name):
    flat = [term for blocks in sums for terms in blocks for term in terms]
    _, rows, width = flat[0][0].shape
    count = len(sums[0])
    steps = 2
    part = rows // steps
    return pl.pallas_call(
        functools.partial(merge_body, [[[0] * len(t) for t in b] for b in sums]),
        grid=(steps,),
        in_specs=[one_block(a, index, part) for a, index in flat],
        out_specs=[pl.BlockSpec((count, part, width), lambda i: (0, i, 0))] * STREAMS,
        out_shape=[jax.ShapeDtypeStruct((count, rows, width), BF)] * STREAMS,
        compiler_params=params(LIMIT),
        cost_estimate=pl.CostEstimate(
            flops=0, transcendentals=0, bytes_accessed=2 * rows * width * (len(flat) + count * STREAMS)
        ),
        name=name,
    )(*[a for a, _ in flat])


def home_body(groups, slots, back_ref, rank_ref, out_ref):
    rows, width = out_ref.shape
    pick = jnp.where(iota((groups * slots, rows), 0) == rank_ref[...], 1.0, 0.0).astype(BF)
    out_ref[...] = dot(pick, back_ref[...].reshape(groups * slots, width), TN).astype(BF)


def home(back, rank):
    groups, slots, width = back.shape
    return pl.pallas_call(
        functools.partial(home_body, groups, slots),
        out_shape=jax.ShapeDtypeStruct((rank.shape[1], width), BF),
        compiler_params=params(LIMIT),
        name="home_rows",
    )(back, rank)


def cut_body(halves, *refs):
    n = len(halves)
    buf, in_sem, out_sem = refs[2 * n :]
    loads = [pltpu.make_async_copy(refs[i].at[h], buf.at[i], in_sem.at[i]) for i, h in enumerate(halves)]
    stores = [pltpu.make_async_copy(buf.at[i], refs[n + i], out_sem.at[i]) for i in range(n)]
    for load in loads:
        load.start()
    for load, store in zip(loads, stores):
        load.wait()
        store.start()
    for store in stores:
        store.wait()


def cut(items):
    n = len(items)
    loose = pl.BlockSpec(memory_space=pltpu.HBM)
    return pl.pallas_call(
        functools.partial(cut_body, [h for _, h in items]),
        in_specs=[loose] * n,
        out_specs=[loose] * n,
        out_shape=[jax.ShapeDtypeStruct(a.shape[1:], a.dtype) for a, _ in items],
        scratch_shapes=[
            pltpu.VMEM((n, *items[0][0].shape[1:]), items[0][0].dtype),
            pltpu.SemaphoreType.DMA((n,)),
            pltpu.SemaphoreType.DMA((n,)),
        ],
        compiler_params=params(LIMIT),
        name="cut_halves",
    )(*[a for a, _ in items])


def work_body(units, n_in, n_out, *refs):
    table_ref, meta_ref, code_hbm, w_hbm, scale_hbm = refs[:5]
    x_refs = refs[5 : 5 + n_in]
    out_refs = refs[5 + n_in : 5 + n_in + n_out]
    signal_ref = refs[5 + n_in + n_out]
    scratch = refs[6 + n_in + n_out :]
    x_buf, out_buf, signal_buf, w_ref, code_ref, lane_scale_ref, state_ref, in_sem, out_sem, signal_sem, w_sem, code_sem = (
        scratch
    )
    total = len(units)
    count, lanes, width = w_ref.shape
    rows = x_buf.shape[1]
    part = rows // 2

    def store(u):
        copies = [pltpu.make_async_copy(signal_buf.at[u], signal_ref.at[u], signal_sem.at[u])]
        for h, (array, block) in enumerate(units[u][1]):
            cut = out_buf.at[u, pl.ds(h * part, part)]
            copies.append(pltpu.make_async_copy(cut, out_refs[array].at[block], out_sem.at[2 * u + h]))
        return copies

    def fetch(u):
        for h, (array, index) in enumerate(units[u][0]):
            cut = x_buf.at[u, pl.ds(h * part, part)]
            pltpu.make_async_copy(x_refs[array].at[index], cut, in_sem.at[u]).start()

    def panel_copies(p):
        return (
            pltpu.make_async_copy(w_hbm.at[p], w_ref.at[p], w_sem.at[p, 0]),
            pltpu.make_async_copy(scale_hbm.at[p], lane_scale_ref.at[p], w_sem.at[p, 1]),
        )

    def ask(panel):
        @pl.when(state_ref[panel] == 0)
        def _():
            state_ref[panel] = 1
            for copy in panel_copies(panel):
                copy.start()

    def need(panel):
        @pl.when(state_ref[panel] == 1)
        def _():
            state_ref[panel] = 2
            for copy in panel_copies(panel):
                copy.wait()

    def slots_of(u):
        batch = meta_ref[0, u]
        first = table_ref[batch, 1]
        second = table_ref[batch, 3]
        use_first = jnp.maximum(first, 0)
        use_second = jnp.where(second >= 0, second, use_first)
        return batch, (first, second), (use_first, use_second)

    code_cut = code_hbm.at[:, 0]
    code_copy = pltpu.make_async_copy(code_cut, code_ref, code_sem.at[0])
    code_copy.start()
    for p in range(count):
        state_ref[p] = 0
    for u in range(total):
        fetch(u)
        for panel in slots_of(u)[2]:
            ask(panel)
    code_copy.wait()

    def ready(u):
        pltpu.make_async_copy(x_buf.at[u], x_buf.at[u], in_sem.at[u]).wait()
        for panel in slots_of(u)[2]:
            need(panel)

    def signals(u):
        batch, asked, use = slots_of(u)
        code = code_ref[batch].astype(F32).astype(jnp.int32)
        code = jnp.where(meta_ref[1, u] == 0, code[: CODE // 2], code[CODE // 2 :])
        scores = dot(jnp.concatenate([w_ref[use[0]], w_ref[use[1]]], axis=0), x_buf[u], NT)
        for c in range(CAP):
            slot = table_ref[batch, 2 * c]
            weight = jnp.where(asked[c] >= 0, 1.0, 0.0)
            scale = jnp.concatenate([lane_scale_ref[use[c]].astype(F32)] * (rows // 128), axis=1)
            score = scores[c * lanes : (c + 1) * lanes] * scale
            lane = iota((lanes, rows), 0)
            hit = lane == jnp.where(code[0:1] == slot, code[4:5], -1)
            for k in range(1, 4):
                hit |= lane == jnp.where(code[k : k + 1] == slot, code[4 + k : 5 + k], -1)
            signal = (jax.nn.sigmoid(score) - jnp.where(hit, 1.0, 0.0)) * (scale * weight)
            signal_buf[u, c] = signal.astype(BF)

    def partial(u):
        use = slots_of(u)[2]
        total_grad = dot(signal_buf[u, 0], w_ref[use[0]], TN) + dot(signal_buf[u, 1], w_ref[use[1]], TN)
        out_buf[u] = total_grad.astype(BF)

    def send(u):
        for v in range(total):

            @pl.when(u == v)
            def _():
                for copy in store(v):
                    copy.start()

    ready(0)
    signals(0)

    def step(u, carry):
        ready(u)
        partial(u - 1)
        signals(u)
        send(u - 1)
        return carry

    lax.fori_loop(1, total, step, 0)
    partial(total - 1)
    for copy in store(total - 1):
        copy.start()
    for u in range(total):
        for copy in store(u):
            copy.wait()


def work(table, offsets, codes, panels, scales, arrays, units, out_blocks, name):
    count, lanes, width = panels.shape
    part = arrays[0].shape[-2]
    rows = 2 * part
    meta = np.array([offsets, [u[2] for u in units]], np.int32)
    total = len(units)
    scalar = pl.BlockSpec(memory_space=pltpu.SMEM)
    loose = pl.BlockSpec(memory_space=pltpu.HBM)
    outs = pl.pallas_call(
        functools.partial(work_body, units, len(arrays), len(out_blocks)),
        in_specs=[scalar, scalar, loose, loose, loose] + [loose] * len(arrays),
        out_specs=[loose] * len(out_blocks) + [loose],
        out_shape=[jax.ShapeDtypeStruct((n, part, width), BF) for n in out_blocks]
        + [jax.ShapeDtypeStruct((total, CAP, lanes, rows), BF)],
        scratch_shapes=[
            pltpu.VMEM((total, rows, width), BF),
            pltpu.VMEM((total, rows, width), BF),
            pltpu.VMEM((total, CAP, lanes, rows), BF),
            pltpu.VMEM(panels.shape, BF),
            pltpu.VMEM((codes.shape[0], CODE, rows), BF),
            pltpu.VMEM(scales.shape, BF),
            pltpu.SMEM((count,), jnp.int32),
            pltpu.SemaphoreType.DMA((total,)),
            pltpu.SemaphoreType.DMA((2 * total,)),
            pltpu.SemaphoreType.DMA((total,)),
            pltpu.SemaphoreType.DMA((count, 2)),
            pltpu.SemaphoreType.DMA((1,)),
        ],
        compiler_params=params(LIMIT),
        cost_estimate=pl.CostEstimate(
            flops=total * 3 * lanes * rows * width * 4,
            transcendentals=0,
            bytes_accessed=panels.size * 2 + total * rows * (width * 4 + lanes * 2),
        ),
        name=name,
    )(table, meta, codes, panels, scales, *arrays)
    return outs[:-1], outs[-1]


def panel_body(parts, n_arrays, n_signals, *refs):
    table_ref = refs[0]
    x_refs = refs[1 : 1 + n_arrays]
    s_refs = refs[1 + n_arrays : 1 + n_arrays + n_signals]
    grad_ref, x_all, s_all, total_ref, grad_buf, x_sem, s_sem, grad_sem = refs[1 + n_arrays + n_signals :]
    rows = x_all.shape[1] // STREAMS
    for rel, pieces in enumerate(parts):
        for pair, (sources, signal, unit) in enumerate(pieces):
            wide = pl.ds(2 * pair * rows, 2 * rows)
            for h, (array, index) in enumerate(sources):
                cut = pl.ds((2 * pair + h) * rows, rows)
                pltpu.make_async_copy(x_refs[array].at[index], x_all.at[rel, cut], x_sem.at[rel]).start()
            pltpu.make_async_copy(s_refs[signal].at[unit], s_all.at[rel, :, :, wide], s_sem.at[rel]).start()
    total_ref[...] = jnp.zeros(total_ref.shape, F32)

    def batch(rel, carry):
        pltpu.make_async_copy(x_all.at[rel], x_all.at[rel], x_sem.at[rel]).wait()
        pltpu.make_async_copy(s_all.at[rel], s_all.at[rel], s_sem.at[rel]).wait()
        first = table_ref[rel, 1]
        second = table_ref[rel, 3]
        lanes = s_all.shape[2]

        @pl.when((first >= 0) & (second < 0))
        def _():
            total_ref[first] += dot(s_all[rel, 0], x_all[rel], NN)

        @pl.when(second >= 0)
        def _():
            both = dot(jnp.concatenate([s_all[rel, 0], s_all[rel, 1]], axis=0), x_all[rel], NN)
            total_ref[first] += both[:lanes]
            total_ref[second] += both[lanes:]

        return carry

    lax.fori_loop(0, len(parts), batch, 0)
    stores = [pltpu.make_async_copy(grad_buf.at[p], grad_ref.at[p], grad_sem.at[p]) for p in range(grad_buf.shape[0])]
    for p, store in enumerate(stores):
        grad_buf[p] = total_ref[p].astype(BF)
        store.start()
    for store in stores:
        store.wait()


def panel_sum(table, arrays, signals, parts, shape):
    count, lanes, width = shape
    rows = arrays[0].shape[2] * STREAMS
    scalar = pl.BlockSpec(memory_space=pltpu.SMEM)
    loose = pl.BlockSpec(memory_space=pltpu.HBM)
    return pl.pallas_call(
        functools.partial(panel_body, parts, len(arrays), len(signals)),
        in_specs=[scalar] + [loose] * (len(arrays) + len(signals)),
        out_specs=loose,
        out_shape=jax.ShapeDtypeStruct(shape, BF),
        scratch_shapes=[
            pltpu.VMEM((len(parts), rows, width), BF),
            pltpu.VMEM((len(parts), CAP, lanes, rows), BF),
            pltpu.VMEM(shape, F32),
            pltpu.VMEM(shape, BF),
            pltpu.SemaphoreType.DMA((len(parts),)),
            pltpu.SemaphoreType.DMA((len(parts),)),
            pltpu.SemaphoreType.DMA((count,)),
        ],
        compiler_params=params(LIMIT),
        cost_estimate=pl.CostEstimate(
            flops=len(parts) * CAP * lanes * rows * width * 2,
            transcendentals=0,
            bytes_accessed=len(parts) * rows * (width + CAP * lanes) * 2 + count * lanes * width * 2,
        ),
        name="panel_grad",
    )(table, *arrays, *signals)


ORDERS = ((1, 3, 4, 12), (3, 1, 12, 4), (4, 12, 1, 3), (12, 4, 3, 1))
STREAMS = len(ORDERS)
RINGS = ((1, 3), (4, 12))
SPREAD = [0]
for mask in ORDERS[0]:
    SPREAD += [r ^ mask for r in SPREAD]


def swap(array, mask, owners):
    return lax.ppermute(array, "label", [(i, i ^ mask) for i in range(owners)])


def shards(queries, cluster_dest, panels, scales, shortlist, positives):
    rows, width = queries.shape
    count, lanes = scales.shape
    groups = lax.axis_size("dp")
    owners = lax.axis_size("label")
    slots = 3 * rows // (2 * groups)
    part = rows // STREAMS
    every = range(STREAMS)
    order = ORDERS
    me = lax.axis_index("label").astype(jnp.int32)

    outgoing, rank = pack(queries, cluster_dest.reshape(1, rows), groups, slots)

    marks = jnp.transpose(positives.reshape(2, 2 * part, -1), (0, 2, 1))
    code = jnp.concatenate([marks // lanes, marks % lanes], axis=1).reshape(CODE, 2 * part)
    listed = jnp.pad(shortlist, ((0, CODE - 1), (0, 2 * part - shortlist.shape[1])))
    code = jnp.stack([code, listed]).astype(F32).astype(BF)[None]
    outgoing, codes = lax.optimization_barrier((outgoing, code))
    arrived = lax.all_to_all(outgoing, "dp", split_axis=0, concat_axis=0, tiled=True)
    for mask in order[0]:
        codes = jnp.concatenate([codes, swap(codes, mask, owners)], axis=0)
    put, *own = land(arrived, codes, rows, slots)
    wanted = codes[:, 1, 0, : shortlist.shape[1]].astype(F32).astype(jnp.int32)

    slot_ids = jnp.arange(wanted.shape[1], dtype=jnp.int32)[None, :]
    mine = wanted // count == me
    local = wanted % count
    first = jnp.min(jnp.where(mine, slot_ids, wanted.shape[1]), axis=1, keepdims=True)
    last = jnp.max(jnp.where(mine, slot_ids, -1), axis=1, keepdims=True)
    first_panel = jnp.max(jnp.where(slot_ids == first, local, -1), axis=1, keepdims=True)
    last_panel = jnp.max(jnp.where(slot_ids == last, local, -1), axis=1, keepdims=True)
    none = first_panel < 0
    single = none | (last == first)
    table = jnp.concatenate(
        [
            jnp.where(none, -1, first),
            first_panel,
            jnp.where(single, -1, last),
            jnp.where(single, -1, last_panel),
        ],
        axis=1,
    )

    arrays = []
    for pair, (one, three) in zip(own, RINGS):
        by1, by3 = swap(pair, one, owners), swap(pair, three, owners)
        low, high = swap(by1[0], three, owners), swap(by3[1], one, owners)
        near = jnp.stack([pair, by1, jnp.stack([low, high]), by3], axis=1)
        arrays.append([near])

    for group, (one, three) in zip(arrays, RINGS[::-1]):
        group += [swap(group[0], one, owners), swap(group[0], three, owners)]
    halves = cut([(group[1 + h], h) for group in arrays for h in (0, 1)])
    for group, (one, three), (low, high) in zip(arrays, RINGS[::-1], (halves[:2], halves[2:])):
        group += [swap(low, three, owners), swap(high, one, owners)]

    def rel(k, bits):
        out = 0
        for s in range(4):
            if bits >> s & 1:
                out ^= order[k][s]
        return out

    where = {}
    wide_scales = jnp.broadcast_to(scales[:, :, None], (count, lanes, 128))

    def bits_of(k, r):
        return next(b for b in range(owners) if rel(k, b) == r)

    def stage(name, index, members):
        outs_of, units, ids, used = {}, [], [], []

        def source(array):
            if array not in used:
                used.append(array)
            return used.index(array)

        for pair, far, spot in members:
            r = 4 * far + spot if pair == 0 else 4 * spot + far
            legs = [(k, bits_of(k, r)) for k in (2 * pair, 2 * pair + 1)]
            if far == 2:
                origin = (((pair, 3), spot), ((pair, 4), spot))
            else:
                array = (pair, (0, 1, None, 2)[far])
                origin = ((array, (0, spot)), (array, (1, spot)))
            for k, b in legs:
                outs_of.setdefault((k, b & 1), []).append(b)
            where[pair, r] = (origin, index, len(units))
            units.append((tuple((source(a), i) for a, i in origin), legs, pair))
            ids.append(SPREAD.index(r))
        keys = sorted(outs_of)
        for key in keys:
            outs_of[key].sort(key=lambda b: (b >> 1 & 1, b))
        units = [
            (origin, tuple((keys.index((k, b & 1)), outs_of[k, b & 1].index(b)) for k, b in legs), pair)
            for origin, legs, pair in units
        ]
        blocks = [len(outs_of[key]) for key in keys]
        ins = [arrays[pair][a] for pair, a in used]
        outs, signals = work(table, ids, codes, panels, wide_scales, ins, units, blocks, name)
        outs = dict(zip(keys, outs))
        for key in keys:
            for n, b in enumerate(outs_of[key]):
                made[key[0], b] = (outs[key], n)
            if key[1]:
                got = swap(outs[key], order[key[0]][0], owners)
                for n, b in enumerate(outs_of[key]):
                    back[key[0], b ^ 1] = (got, n)
        return signals

    made = {}
    back = {}

    ahead = (1, 2, 3)
    signals = [
        stage("work_near", 0, [(q, 0, p) for p in ahead for q in (0, 1)]),
        stage("work_far", 1, [(q, f, p) for f in (1, 3) for p in ahead for q in (0, 1)]),
        stage("work_last", 2, [(q, 2, p) for p in ahead for q in (0, 1)]),
        stage("work_kept", 3, [(q, f, 0) for f in (0, 1, 3, 2) for q in (0, 1)]),
    ]

    def terms(k, b):
        return [made[k, b], back[k, b]] + [(got, bits.index(b)) for got, bits in later[k] if b in bits]

    later = {k: [] for k in every}
    for step in (1, 2, 3):
        bit = 1 << step
        sent = [b for b in range(owners) if b & bit and not b & (bit - 1)]
        sums = merge([[terms(k, b) for b in sent] for k in every], f"merge_{step}")
        for k in every:
            later[k].append((swap(sums[k], order[k][step], owners), [b ^ bit for b in sent]))
    leaving = leave(put, [terms(k, 0) for k in every], groups)
    returned = lax.all_to_all(leaving, "dp", split_axis=0, concat_axis=0, tiled=True)

    flat = [(pair, a) for pair in (0, 1) for a in range(5)]
    parts = []
    for r in SPREAD:
        parts.append([])
        for pair in (0, 1):
            origin, signal, unit = where[pair, r]
            parts[-1].append((tuple((flat.index(a), i) for a, i in origin), signal, unit))
    panel_grad = panel_sum(
        table,
        [arrays[pair][a] for pair, a in flat],
        signals,
        parts,
        panels.shape,
    )
    return home(returned, rank), panel_grad


def solution(mesh):
    placed = (
        P(("dp", "label"), None),
        P(("dp", "label")),
        P(("dp", "label"), None, None),
        P(("dp", "label"), None),
        P(("dp", "label"), None),
        P(("dp", "label"), None),
    )
    return jax.shard_map(
        shards,
        mesh=mesh,
        in_specs=placed,
        out_specs=(P(("dp", "label"), None), P(("dp", "label"), None, None)),
        check_vma=False,
    )
```

```python
import functools
import jax
import jax.numpy as jnp
import numpy as np
from jax import lax
from jax.experimental import pallas as pl
from jax.experimental.pallas import tpu as pltpu
from jax.sharding import PartitionSpec as P

CAP = 2
CODE = 16
LIMIT = 63 << 20
BF = jnp.bfloat16
F32 = jnp.float32


def iota(shape, axis):
    return lax.broadcasted_iota(jnp.int32, shape, axis)


def dot(a, b, dims):
    return lax.dot_general(a, b, (dims, ((), ())), preferred_element_type=F32)


NN = ((1,), (0,))
NT = ((1,), (1,))
TN = ((0,), (0,))


def params(limit):
    return pltpu.CompilerParams(vmem_limit_bytes=limit)


def pack_body(groups, slots, x_ref, dest_ref, out_ref, rank_ref):
    rows = x_ref.shape[0]
    dest = dest_ref[...]
    target = dest // rows
    place = dest % rows
    member = jnp.where(iota((16, rows), 0) == target, 1.0, 0.0)
    earlier = jnp.where(iota((rows, rows), 0) < iota((rows, rows), 1), 1.0, 0.0).astype(BF)
    rank = jnp.sum(dot(member.astype(BF), earlier, NN) * member, axis=0, keepdims=True)
    rank = rank.astype(jnp.int32)
    rank_ref[...] = rank + target * slots
    kind = iota((CODE, rows), 0)
    code = jnp.where(kind == 0, place // 16, jnp.where(kind == 1, place % 16, 1))
    code = code.astype(F32).astype(BF)
    out_ref[:, slots:, :] = jnp.zeros((groups, CODE, x_ref.shape[1]), BF)
    for t in range(groups):
        pick = jnp.where(iota((slots, rows), 0) == jnp.where(target == t, rank, -1), 1.0, 0.0).astype(BF)
        out_ref[t, :slots, :] = dot(pick, x_ref[...], NN).astype(BF)
        out_ref[t, slots:, :slots] = dot(code, pick, NT).astype(BF)


def pack(x, dest, groups, slots):
    rows, width = x.shape
    return pl.pallas_call(
        functools.partial(pack_body, groups, slots),
        out_shape=(
            jax.ShapeDtypeStruct((groups, slots + CODE, width), BF),
            jax.ShapeDtypeStruct((1, rows), jnp.int32),
        ),
        compiler_params=params(LIMIT),
        name="pack_rows",
    )(x, dest)


def land_body(groups, slots, arrived_ref, code_ref, put_ref, *pair_refs):
    part = pair_refs[0].shape[1]
    rows = 2 * part * len(pair_refs)
    width = arrived_ref.shape[2]
    for s in range(groups):
        code = jnp.transpose(arrived_ref[s, slots:, :128].astype(F32))[:slots]
        place = jnp.where(code[:, 2:3] > 0.5, code[:, 0:1] * 16.0 + code[:, 1:2], -1.0).astype(jnp.int32)
        put = jnp.where(iota((slots, rows), 1) == place, 1.0, 0.0).astype(BF)
        put_ref[s * slots : (s + 1) * slots, :] = put
    sent = arrived_ref[:, :slots, :].reshape(groups * slots, width)
    total = dot(put_ref[...], sent, TN)
    for k in range(2 * len(pair_refs)):
        pair_refs[k // 2][k % 2] = total[k * part : (k + 1) * part].astype(BF)


def land(arrived, codes, rows, slots):
    groups, _, width = arrived.shape
    pair = jax.ShapeDtypeStruct((2, rows // STREAMS, width), BF)
    return pl.pallas_call(
        functools.partial(land_body, groups, slots),
        in_specs=[pl.BlockSpec(memory_space=pltpu.VMEM), pl.BlockSpec(memory_space=pltpu.HBM)],
        out_shape=(jax.ShapeDtypeStruct((groups * slots, rows), BF), pair, pair),
        compiler_params=params(LIMIT),
        name="land_rows",
    )(arrived, codes)


def leave_body(groups, slots, terms, *refs):
    put_ref, out_ref = refs[0], refs[-1]
    streams = []
    for k in range(STREAMS):
        total = refs[1 + k * terms][0].astype(F32)
        for ref in refs[2 + k * terms : 1 + (k + 1) * terms]:
            total += ref[0].astype(F32)
        streams.append(total.astype(BF))
    grad = jnp.concatenate(streams, axis=0)
    out_ref[...] = dot(put_ref[...], grad, NN).astype(BF).reshape(groups, slots, grad.shape[1])


def one_block(array, index, part):
    _, rows, width = array.shape
    return pl.BlockSpec((1, part, width), lambda i: (index, i, 0))


def leave(put, terms, groups):
    slots = put.shape[0] // groups
    flat = [term for stream in terms for term in stream]
    width = flat[0][0].shape[2]
    return pl.pallas_call(
        functools.partial(leave_body, groups, slots, len(terms[0])),
        grid=(1,),
        in_specs=[pl.BlockSpec(put.shape, lambda i: (0, 0))]
        + [one_block(a, index, a.shape[1]) for a, index in flat],
        out_specs=pl.BlockSpec((groups, slots, width), lambda i: (0, 0, 0)),
        out_shape=jax.ShapeDtypeStruct((groups, slots, width), BF),
        compiler_params=params(LIMIT),
        name="leave_rows",
    )(put, *[a for a, _ in flat])


def merge_body(sums, *refs):
    outs = refs[-STREAMS:]
    at = 0
    for k, blocks in enumerate(sums):
        for j, terms in enumerate(blocks):
            total = refs[at][0].astype(F32)
            for ref in refs[at + 1 : at + len(terms)]:
                total += ref[0].astype(F32)
            outs[k][j] = total.astype(BF)
            at += len(terms)


def merge(sums, name):
    flat = [term for blocks in sums for terms in blocks for term in terms]
    _, rows, width = flat[0][0].shape
    count = len(sums[0])
    steps = 2
    part = rows // steps
    return pl.pallas_call(
        functools.partial(merge_body, [[[0] * len(t) for t in b] for b in sums]),
        grid=(steps,),
        in_specs=[one_block(a, index, part) for a, index in flat],
        out_specs=[pl.BlockSpec((count, part, width), lambda i: (0, i, 0))] * STREAMS,
        out_shape=[jax.ShapeDtypeStruct((count, rows, width), BF)] * STREAMS,
        compiler_params=params(LIMIT),
        cost_estimate=pl.CostEstimate(
            flops=0, transcendentals=0, bytes_accessed=2 * rows * width * (len(flat) + count * STREAMS)
        ),
        name=name,
    )(*[a for a, _ in flat])


def home_body(groups, slots, back_ref, rank_ref, out_ref):
    rows, width = out_ref.shape
    pick = jnp.where(iota((groups * slots, rows), 0) == rank_ref[...], 1.0, 0.0).astype(BF)
    out_ref[...] = dot(pick, back_ref[...].reshape(groups * slots, width), TN).astype(BF)


def home(back, rank):
    groups, slots, width = back.shape
    return pl.pallas_call(
        functools.partial(home_body, groups, slots),
        out_shape=jax.ShapeDtypeStruct((rank.shape[1], width), BF),
        compiler_params=params(LIMIT),
        name="home_rows",
    )(back, rank)


def cut_body(halves, *refs):
    n = len(halves)
    buf, in_sem, out_sem = refs[2 * n :]
    loads = [pltpu.make_async_copy(refs[i].at[h], buf.at[i], in_sem.at[i]) for i, h in enumerate(halves)]
    stores = [pltpu.make_async_copy(buf.at[i], refs[n + i], out_sem.at[i]) for i in range(n)]
    for load in loads:
        load.start()
    for load, store in zip(loads, stores):
        load.wait()
        store.start()
    for store in stores:
        store.wait()


def cut(items):
    n = len(items)
    loose = pl.BlockSpec(memory_space=pltpu.HBM)
    return pl.pallas_call(
        functools.partial(cut_body, [h for _, h in items]),
        in_specs=[loose] * n,
        out_specs=[loose] * n,
        out_shape=[jax.ShapeDtypeStruct(a.shape[1:], a.dtype) for a, _ in items],
        scratch_shapes=[
            pltpu.VMEM((n, *items[0][0].shape[1:]), items[0][0].dtype),
            pltpu.SemaphoreType.DMA((n,)),
            pltpu.SemaphoreType.DMA((n,)),
        ],
        compiler_params=params(LIMIT),
        name="cut_halves",
    )(*[a for a, _ in items])


def work_body(units, n_in, n_out, *refs):
    table_ref, meta_ref, code_hbm, w_hbm, scale_hbm = refs[:5]
    x_refs = refs[5 : 5 + n_in]
    out_refs = refs[5 + n_in : 5 + n_in + n_out]
    signal_ref = refs[5 + n_in + n_out]
    scratch = refs[6 + n_in + n_out :]
    x_buf, out_buf, signal_buf, w_ref, code_ref, lane_scale_ref, state_ref, in_sem, out_sem, signal_sem, w_sem, code_sem = (
        scratch
    )
    total = len(units)
    count, lanes, width = w_ref.shape
    rows = x_buf.shape[1]
    part = rows // 2

    def store(u):
        copies = [pltpu.make_async_copy(signal_buf.at[u], signal_ref.at[u], signal_sem.at[u])]
        for h, (array, block) in enumerate(units[u][1]):
            cut = out_buf.at[u, pl.ds(h * part, part)]
            copies.append(pltpu.make_async_copy(cut, out_refs[array].at[block], out_sem.at[2 * u + h]))
        return copies

    def fetch(u):
        for h, (array, index) in enumerate(units[u][0]):
            cut = x_buf.at[u, pl.ds(h * part, part)]
            pltpu.make_async_copy(x_refs[array].at[index], cut, in_sem.at[u]).start()

    def panel_copies(p):
        return (
            pltpu.make_async_copy(w_hbm.at[p], w_ref.at[p], w_sem.at[p, 0]),
            pltpu.make_async_copy(scale_hbm.at[p], lane_scale_ref.at[p], w_sem.at[p, 1]),
        )

    def ask(panel):
        @pl.when(state_ref[panel] == 0)
        def _():
            state_ref[panel] = 1
            for copy in panel_copies(panel):
                copy.start()

    def need(panel):
        @pl.when(state_ref[panel] == 1)
        def _():
            state_ref[panel] = 2
            for copy in panel_copies(panel):
                copy.wait()

    def slots_of(u):
        batch = meta_ref[0, u]
        first = table_ref[batch, 1]
        second = table_ref[batch, 3]
        use_first = jnp.maximum(first, 0)
        use_second = jnp.where(second >= 0, second, use_first)
        return batch, (first, second), (use_first, use_second)

    code_cut = code_hbm.at[:, 0]
    code_copy = pltpu.make_async_copy(code_cut, code_ref, code_sem.at[0])
    code_copy.start()
    for p in range(count):
        state_ref[p] = 0
    for u in range(total):
        fetch(u)
        for panel in slots_of(u)[2]:
            ask(panel)
    code_copy.wait()

    def ready(u):
        pltpu.make_async_copy(x_buf.at[u], x_buf.at[u], in_sem.at[u]).wait()
        for panel in slots_of(u)[2]:
            need(panel)

    def signals(u):
        batch, asked, use = slots_of(u)
        code = code_ref[batch].astype(F32).astype(jnp.int32)
        code = jnp.where(meta_ref[1, u] == 0, code[: CODE // 2], code[CODE // 2 :])
        scores = dot(jnp.concatenate([w_ref[use[0]], w_ref[use[1]]], axis=0), x_buf[u], NT)
        for c in range(CAP):
            slot = table_ref[batch, 2 * c]
            weight = jnp.where(asked[c] >= 0, 1.0, 0.0)
            scale = jnp.concatenate([lane_scale_ref[use[c]].astype(F32)] * (rows // 128), axis=1)
            score = scores[c * lanes : (c + 1) * lanes] * scale
            lane = iota((lanes, rows), 0)
            hit = lane == jnp.where(code[0:1] == slot, code[4:5], -1)
            for k in range(1, 4):
                hit |= lane == jnp.where(code[k : k + 1] == slot, code[4 + k : 5 + k], -1)
            signal = (jax.nn.sigmoid(score) - jnp.where(hit, 1.0, 0.0)) * (scale * weight)
            signal_buf[u, c] = signal.astype(BF)

    def partial(u):
        use = slots_of(u)[2]
        total_grad = dot(signal_buf[u, 0], w_ref[use[0]], TN) + dot(signal_buf[u, 1], w_ref[use[1]], TN)
        out_buf[u] = total_grad.astype(BF)

    def send(u):
        for v in range(total):

            @pl.when(u == v)
            def _():
                for copy in store(v):
                    copy.start()

    ready(0)
    signals(0)

    def step(u, carry):
        ready(u)
        partial(u - 1)
        signals(u)
        send(u - 1)
        return carry

    if total <= 6:
        for u in range(1, total):
            ready(u)
            partial(u - 1)
            signals(u)
            for copy in store(u - 1):
                copy.start()
    else:
        lax.fori_loop(1, total, step, 0)
    partial(total - 1)
    for copy in store(total - 1):
        copy.start()
    for u in range(total):
        for copy in store(u):
            copy.wait()


def work(table, offsets, codes, panels, scales, arrays, units, out_blocks, name):
    count, lanes, width = panels.shape
    part = arrays[0].shape[-2]
    rows = 2 * part
    meta = np.array([offsets, [u[2] for u in units]], np.int32)
    total = len(units)
    scalar = pl.BlockSpec(memory_space=pltpu.SMEM)
    loose = pl.BlockSpec(memory_space=pltpu.HBM)
    outs = pl.pallas_call(
        functools.partial(work_body, units, len(arrays), len(out_blocks)),
        in_specs=[scalar, scalar, loose, loose, loose] + [loose] * len(arrays),
        out_specs=[loose] * len(out_blocks) + [loose],
        out_shape=[jax.ShapeDtypeStruct((n, part, width), BF) for n in out_blocks]
        + [jax.ShapeDtypeStruct((total, CAP, lanes, rows), BF)],
        scratch_shapes=[
            pltpu.VMEM((total, rows, width), BF),
            pltpu.VMEM((total, rows, width), BF),
            pltpu.VMEM((total, CAP, lanes, rows), BF),
            pltpu.VMEM(panels.shape, BF),
            pltpu.VMEM((codes.shape[0], CODE, rows), BF),
            pltpu.VMEM(scales.shape, BF),
            pltpu.SMEM((count,), jnp.int32),
            pltpu.SemaphoreType.DMA((total,)),
            pltpu.SemaphoreType.DMA((2 * total,)),
            pltpu.SemaphoreType.DMA((total,)),
            pltpu.SemaphoreType.DMA((count, 2)),
            pltpu.SemaphoreType.DMA((1,)),
        ],
        compiler_params=params(LIMIT),
        cost_estimate=pl.CostEstimate(
            flops=total * 3 * lanes * rows * width * 4,
            transcendentals=0,
            bytes_accessed=panels.size * 2 + total * rows * (width * 4 + lanes * 2),
        ),
        name=name,
    )(table, meta, codes, panels, scales, *arrays)
    return outs[:-1], outs[-1]


def panel_body(parts, n_arrays, n_signals, *refs):
    table_ref = refs[0]
    x_refs = refs[1 : 1 + n_arrays]
    s_refs = refs[1 + n_arrays : 1 + n_arrays + n_signals]
    grad_ref, x_all, s_all, total_ref, x_sem, s_sem = refs[1 + n_arrays + n_signals :]
    rows = x_all.shape[1] // STREAMS
    for rel, pieces in enumerate(parts):
        for pair, (sources, signal, unit) in enumerate(pieces):
            wide = pl.ds(2 * pair * rows, 2 * rows)
            for h, (array, index) in enumerate(sources):
                cut = pl.ds((2 * pair + h) * rows, rows)
                pltpu.make_async_copy(x_refs[array].at[index], x_all.at[rel, cut], x_sem.at[rel]).start()
            pltpu.make_async_copy(s_refs[signal].at[unit], s_all.at[rel, :, :, wide], s_sem.at[rel]).start()
    total_ref[...] = jnp.zeros(total_ref.shape, F32)

    def batch(rel, carry):
        pltpu.make_async_copy(x_all.at[rel], x_all.at[rel], x_sem.at[rel]).wait()
        pltpu.make_async_copy(s_all.at[rel], s_all.at[rel], s_sem.at[rel]).wait()
        first = table_ref[rel, 1]
        second = table_ref[rel, 3]
        lanes = s_all.shape[2]

        @pl.when((first >= 0) & (second < 0))
        def _():
            total_ref[first] += dot(s_all[rel, 0], x_all[rel], NN)

        @pl.when(second >= 0)
        def _():
            both = dot(jnp.concatenate([s_all[rel, 0], s_all[rel, 1]], axis=0), x_all[rel], NN)
            total_ref[first] += both[:lanes]
            total_ref[second] += both[lanes:]

        return carry

    lax.fori_loop(0, len(parts), batch, 0)
    grad_ref[...] = total_ref[...].astype(BF)


def panel_sum(table, arrays, signals, parts, shape):
    count, lanes, width = shape
    rows = arrays[0].shape[2] * STREAMS
    scalar = pl.BlockSpec(memory_space=pltpu.SMEM)
    loose = pl.BlockSpec(memory_space=pltpu.HBM)
    return pl.pallas_call(
        functools.partial(panel_body, parts, len(arrays), len(signals)),
        in_specs=[scalar] + [loose] * (len(arrays) + len(signals)),
        out_specs=pl.BlockSpec(memory_space=pltpu.VMEM),
        out_shape=jax.ShapeDtypeStruct(shape, BF),
        scratch_shapes=[
            pltpu.VMEM((len(parts), rows, width), BF),
            pltpu.VMEM((len(parts), CAP, lanes, rows), BF),
            pltpu.VMEM(shape, F32),
            pltpu.SemaphoreType.DMA((len(parts),)),
            pltpu.SemaphoreType.DMA((len(parts),)),
        ],
        compiler_params=params(LIMIT),
        cost_estimate=pl.CostEstimate(
            flops=len(parts) * CAP * lanes * rows * width * 2,
            transcendentals=0,
            bytes_accessed=len(parts) * rows * (width + CAP * lanes) * 2 + count * lanes * width * 2,
        ),
        name="panel_grad",
    )(table, *arrays, *signals)


ORDERS = ((1, 3, 4, 12), (3, 1, 12, 4), (4, 12, 1, 3), (12, 4, 3, 1))
STREAMS = len(ORDERS)
RINGS = ((1, 3), (4, 12))
SPREAD = [0]
for mask in ORDERS[0]:
    SPREAD += [r ^ mask for r in SPREAD]


def swap(array, mask, owners):
    return lax.ppermute(array, "label", [(i, i ^ mask) for i in range(owners)])


def shards(queries, cluster_dest, panels, scales, shortlist, positives):
    rows, width = queries.shape
    count, lanes = scales.shape
    groups = lax.axis_size("dp")
    owners = lax.axis_size("label")
    slots = 3 * rows // (2 * groups)
    part = rows // STREAMS
    every = range(STREAMS)
    order = ORDERS
    me = lax.axis_index("label").astype(jnp.int32)

    outgoing, rank = pack(queries, cluster_dest.reshape(1, rows), groups, slots)

    marks = jnp.transpose(positives.reshape(2, 2 * part, -1), (0, 2, 1))
    code = jnp.concatenate([marks // lanes, marks % lanes], axis=1).reshape(CODE, 2 * part)
    listed = jnp.pad(shortlist, ((0, CODE - 1), (0, 2 * part - shortlist.shape[1])))
    code = jnp.stack([code, listed]).astype(F32).astype(BF)[None]
    outgoing, codes = lax.optimization_barrier((outgoing, code))
    arrived = lax.all_to_all(outgoing, "dp", split_axis=0, concat_axis=0, tiled=True)
    for mask in order[0]:
        codes = jnp.concatenate([codes, swap(codes, mask, owners)], axis=0)
    put, *own = land(arrived, codes, rows, slots)
    wanted = codes[:, 1, 0, : shortlist.shape[1]].astype(F32).astype(jnp.int32)

    slot_ids = jnp.arange(wanted.shape[1], dtype=jnp.int32)[None, :]
    mine = wanted // count == me
    local = wanted % count
    first = jnp.min(jnp.where(mine, slot_ids, wanted.shape[1]), axis=1, keepdims=True)
    last = jnp.max(jnp.where(mine, slot_ids, -1), axis=1, keepdims=True)
    first_panel = jnp.max(jnp.where(slot_ids == first, local, -1), axis=1, keepdims=True)
    last_panel = jnp.max(jnp.where(slot_ids == last, local, -1), axis=1, keepdims=True)
    none = first_panel < 0
    single = none | (last == first)
    table = jnp.concatenate(
        [
            jnp.where(none, -1, first),
            first_panel,
            jnp.where(single, -1, last),
            jnp.where(single, -1, last_panel),
        ],
        axis=1,
    )

    arrays = []
    for pair, (one, three) in zip(own, RINGS):
        by1, by3 = swap(pair, one, owners), swap(pair, three, owners)
        low, high = swap(by1[0], three, owners), swap(by3[1], one, owners)
        near = jnp.stack([pair, by1, jnp.stack([low, high]), by3], axis=1)
        arrays.append([near])

    for group, (one, three) in zip(arrays, RINGS[::-1]):
        group += [swap(group[0], one, owners), swap(group[0], three, owners)]
    halves = cut([(group[1 + h], h) for group in arrays for h in (0, 1)])
    for group, (one, three), (low, high) in zip(arrays, RINGS[::-1], (halves[:2], halves[2:])):
        group += [swap(low, three, owners), swap(high, one, owners)]

    def rel(k, bits):
        out = 0
        for s in range(4):
            if bits >> s & 1:
                out ^= order[k][s]
        return out

    where = {}
    wide_scales = jnp.broadcast_to(scales[:, :, None], (count, lanes, 128))

    def bits_of(k, r):
        return next(b for b in range(owners) if rel(k, b) == r)

    def stage(name, index, members):
        outs_of, units, ids, used = {}, [], [], []

        def source(array):
            if array not in used:
                used.append(array)
            return used.index(array)

        for pair, far, spot in members:
            r = 4 * far + spot if pair == 0 else 4 * spot + far
            legs = [(k, bits_of(k, r)) for k in (2 * pair, 2 * pair + 1)]
            if far == 2:
                origin = (((pair, 3), spot), ((pair, 4), spot))
            else:
                array = (pair, (0, 1, None, 2)[far])
                origin = ((array, (0, spot)), (array, (1, spot)))
            for k, b in legs:
                outs_of.setdefault((k, b & 1), []).append(b)
            where[pair, r] = (origin, index, len(units))
            units.append((tuple((source(a), i) for a, i in origin), legs, pair))
            ids.append(SPREAD.index(r))
        keys = sorted(outs_of)
        for key in keys:
            outs_of[key].sort(key=lambda b: (b >> 1 & 1, b))
        units = [
            (origin, tuple((keys.index((k, b & 1)), outs_of[k, b & 1].index(b)) for k, b in legs), pair)
            for origin, legs, pair in units
        ]
        blocks = [len(outs_of[key]) for key in keys]
        ins = [arrays[pair][a] for pair, a in used]
        outs, signals = work(table, ids, codes, panels, wide_scales, ins, units, blocks, name)
        outs = dict(zip(keys, outs))
        for key in keys:
            for n, b in enumerate(outs_of[key]):
                made[key[0], b] = (outs[key], n)
            if key[1]:
                got = swap(outs[key], order[key[0]][0], owners)
                for n, b in enumerate(outs_of[key]):
                    back[key[0], b ^ 1] = (got, n)
        return signals

    made = {}
    back = {}

    ahead = (1, 2, 3)
    signals = [
        stage("work_near", 0, [(q, 0, p) for p in ahead for q in (0, 1)]),
        stage("work_far", 1, [(q, f, p) for f in (1, 3) for p in ahead for q in (0, 1)]),
        stage("work_last", 2, [(q, 2, p) for p in ahead for q in (0, 1)]),
        stage("work_kept", 3, [(q, f, 0) for f in (0, 1, 3, 2) for q in (0, 1)]),
    ]

    def terms(k, b):
        return [made[k, b], back[k, b]] + [(got, bits.index(b)) for got, bits in later[k] if b in bits]

    later = {k: [] for k in every}
    for step in (1, 2, 3):
        bit = 1 << step
        sent = [b for b in range(owners) if b & bit and not b & (bit - 1)]
        sums = merge([[terms(k, b) for b in sent] for k in every], f"merge_{step}")
        for k in every:
            later[k].append((swap(sums[k], order[k][step], owners), [b ^ bit for b in sent]))
    leaving = leave(put, [terms(k, 0) for k in every], groups)
    returned = lax.all_to_all(leaving, "dp", split_axis=0, concat_axis=0, tiled=True)

    flat = [(pair, a) for pair in (0, 1) for a in range(5)]
    parts = []
    for r in SPREAD:
        parts.append([])
        for pair in (0, 1):
            origin, signal, unit = where[pair, r]
            parts[-1].append((tuple((flat.index(a), i) for a, i in origin), signal, unit))
    panel_grad = panel_sum(
        table,
        [arrays[pair][a] for pair, a in flat],
        signals,
        parts,
        panels.shape,
    )
    return home(returned, rank), panel_grad


def solution(mesh):
    placed = (
        P(("dp", "label"), None),
        P(("dp", "label")),
        P(("dp", "label"), None, None),
        P(("dp", "label"), None),
        P(("dp", "label"), None),
        P(("dp", "label"), None),
    )
    return jax.shard_map(
        shards,
        mesh=mesh,
        in_specs=placed,
        out_specs=(P(("dp", "label"), None), P(("dp", "label"), None, None)),
        check_vma=False,
    )
```
